256 devices in a mesh: slab: 16 (over z, core), dom: 16 (over y, x).
Axes of the slice: x: 4, y: 4, z: 8, core: 2. Of those that a mesh axis runs over, the one named last changes fastest.
Arguments:
- a_blocks: bfloat16 [32768, 7, 4096], P(('slab', 'dom')), may hold values from -5 to 5
- p_blocks: bfloat16 [32768, 4096], P(('slab', 'dom')), may hold values from -0.75 to 0.75
- dest_rank: int32 [229376, 1], P(('slab', 'dom')), may hold values from 0 to 15; in each aligned block of 896 rows (0 to 895, 896 to 1791, ...) at most 112 rows name the same one
- dest_block: int32 [32768, 7], P(('slab', 'dom')), may hold values from 0 to 127
Outputs:
- coarse: float32 [32768, 4096], P(('slab', 'dom'))
The draws below stay inside these ranges and needn't reach their ends.
Inputs may be any that keep to these rules, and one draw needn't show every extreme that they name: `dest_rank`: among the 896 rows of one device no owner index appears more than 112 times, and some owner index appears exactly 112 times.
All inputs are finite; a program needn't handle non-finite values.
Results may differ from the reference program's by a relative error of at most 0.0041.
Values may be sent and summed in bfloat16 or wider, within the bound.
No kernel may reach another device: no remote copies, remote signals or barrier semaphores. Data moves between devices by JAX's collectives and lax.ppermute only.
A program may use at most 128 MiB of HBM per device.

```python
import math
import jax
import jax.numpy as jnp
import numpy as np
from jax import lax

BLOCK = 64
PAIRS = 7
EX = 8
EY = 4
EZ = 4
CB_DEV = 128
E_DEV = 128
ELEMS = 32768
NZ = 64
NY = 64
CAP = 112
CB_TOTAL = 32768
N_DOM = 16


def set_ends(array, rng, low, high):
    index_at = [jax.random.randint(jax.random.fold_in(rng, axis), (), 0, length) for axis, length in enumerate(array.shape)]
    widest = array.shape.index(max(array.shape))
    next_to = index_at[:widest] + [(index_at[widest] + 1) % array.shape[widest]] + index_at[widest + 1:]
    return array.at[tuple(index_at)].set(low).at[tuple(next_to)].set(high)


def block_levels(rng, extent, cuts, low, high):
    def one(dim, shards_of):
        draws = jax.random.uniform(jax.random.fold_in(jax.random.fold_in(rng, 6), dim), (shards_of,), jnp.float32, low / len(cuts), high / len(cuts))
        return jnp.repeat(jnp.exp(draws), extent[dim] // shards_of).reshape((-1,) + (1,) * (len(extent) - dim - 1))

    gain = one(*cuts[0])
    for cut in cuts[1:]:
        gain = gain * one(*cut)
    return gain


def assign_block(stream_key, own, number, rows, number_of, top, bound, lean):
    order = jax.random.permutation(stream_key, number_of)
    packed, ordinary = portions_of(number_of, rows * top, bound, lean, True), portions_of(number_of, rows * top, bound, lean, False)
    places = jnp.arange(number_of)

    def named(tallies, turn):
        used = int((tallies > 0).sum())
        fixed = max(1, used // 4)
        passed = fixed + (places - fixed + turn * (used - fixed)) % max(1, number_of - fixed)
        return jnp.zeros((number_of,), jnp.int32).at[order[jnp.where(places < fixed, places, passed)]].set(jnp.asarray(tallies, jnp.int32))

    tallies = jnp.where(number % 4 == 0, named(packed, number // 4), named(ordinary, number - number // 4 - 1))
    mixed = jax.random.permutation(jax.random.fold_in(own, 3), number_of)
    source_of, taker = mixed[0:number_of // 2 * 2:2], mixed[1:number_of // 2 * 2:2]
    slack = jnp.minimum(tallies[source_of] - 1, bound - tallies[taker]) // 2
    slack = jnp.where((source_of == order[0]) | (taker == order[0]) | (tallies[taker] == 0), 0, jnp.maximum(slack, 0))
    passed = jax.random.randint(jax.random.fold_in(own, 4), (number_of // 2,), 0, 1 << 20) % (slack + 1)
    tallies = tallies.at[source_of].add(-passed).at[taker].add(passed)
    labels = jnp.searchsorted(jnp.cumsum(tallies), jnp.arange(rows * top), side="right").astype(jnp.int32)
    table = labels.reshape(top, rows).T
    table = table[jax.random.permutation(jax.random.fold_in(own, 1), rows)]
    turn = jax.random.randint(jax.random.fold_in(own, 2), (rows, 1), 0, top)
    return jnp.take_along_axis(table, (jnp.arange(top)[None, :] + turn) % top, axis=1)


def portions_of(count, total, bound, skew, full):
    loads = [(1 << 20) // math.isqrt(standing ** skew) + 1 for standing in range(1, count + 1)]
    largest = bound if full else min(bound, max(-(-total // count), total * loads[0] // sum(loads)))
    least = 1 if total - largest >= count - 1 else 0
    holding, rest = [largest] + [least] * (count - 1), total - largest - least * (count - 1)
    while rest > 0:
        movable = [i for i in range(1, count) if holding[i] < largest] or [i for i in range(1, count) if holding[i] < bound]
        pool, remaining = sum([loads[i] for i in movable]), rest
        for i in movable:
            more = min(bound - holding[i], max(1, remaining * loads[i] // pool), rest)
            holding[i] = holding[i] + more
            rest = rest - more
    return np.array(holding)


def gaussian(stream_key, extent, spread, bound, split=(), kind=jnp.bfloat16):
    factor_of = block_levels(stream_key, extent, split, -0.22, 0.18) if split else 1.0
    drawn = jax.random.normal(stream_key, extent, jnp.float32) * spread * factor_of
    return jnp.minimum(jnp.maximum(drawn, -bound), bound).astype(kind)


def setup_inputs(seed: int = 0) -> dict:
    key_of = jax.random.split(jax.random.key(seed), 5)
    a_blocks = gaussian(key_of[0], (ELEMS, PAIRS, BLOCK * BLOCK), 0.35, 5.0, ((0, 256),))
    p_blocks = gaussian(key_of[1], (ELEMS, BLOCK * BLOCK), BLOCK ** -0.5, 0.75, ((0, 256),))
    dest_rank_keys = jax.random.split(jax.random.fold_in(key_of[2], 1), (ELEMS * PAIRS) // (E_DEV * PAIRS))
    dest_rank_turns = jax.random.permutation(jax.random.fold_in(key_of[2], 3), (ELEMS * PAIRS) // (E_DEV * PAIRS))
    dest_rank = jax.vmap(lambda own, number: assign_block(jax.random.fold_in(key_of[2], 2), own, number, E_DEV * PAIRS, N_DOM, 1, CAP, 1))(dest_rank_keys, dest_rank_turns).reshape((ELEMS * PAIRS, 1))
    dest_block = set_ends(jax.random.randint(key_of[3], (ELEMS, PAIRS), 0, CB_DEV), jax.random.fold_in(key_of[3], 1), 0, CB_DEV - 1).astype(jnp.int32)
    return {"a_blocks": a_blocks, "p_blocks": p_blocks, "dest_rank": dest_rank, "dest_block": dest_block}


def neighbour_stack(padded):
    middle = padded[1:-1, 1:-1, 1:-1]
    return jnp.stack([middle, padded[1:-1, 1:-1, :-2], padded[1:-1, 1:-1, 2:],
                      padded[1:-1, :-2, 1:-1], padded[1:-1, 2:, 1:-1],
                      padded[:-2, 1:-1, 1:-1], padded[2:, 1:-1, 1:-1]], axis=3)


def reference(a_blocks, p_blocks, dest_rank, dest_block):
    slab_count = NZ // EZ
    domains = NY // EY
    per_device = EZ * EY * EX
    square = BLOCK * BLOCK
    layout = p_blocks.reshape(slab_count, domains, EZ, EY, EX, square)
    layout = layout.transpose(0, 2, 1, 3, 4, 5).reshape(NZ, NY, EX, square)
    padded = jnp.pad(layout, ((1, 1), (1, 1), (1, 1), (0, 0)))
    owner_rank = dest_rank.reshape(-1)
    target_block = dest_block.reshape(-1)

    def device_step(coarse, index):
        slab_index = index // domains
        domain = index % domains
        start = (index * per_device).astype(jnp.int32)
        brick_rows = lax.dynamic_slice(padded, ((slab_index * EZ).astype(jnp.int32), (domain * EY).astype(jnp.int32), jnp.int32(0), jnp.int32(0)), (EZ + 2, EY + 2, EX + 2, square))
        beside = neighbour_stack(brick_rows).reshape(per_device, PAIRS, BLOCK, BLOCK).astype(jnp.float32)
        couple = lax.dynamic_slice_in_dim(a_blocks, start, per_device, 0).reshape(per_device, PAIRS, BLOCK, BLOCK).astype(jnp.float32)
        self_rows = lax.dynamic_slice_in_dim(p_blocks, start, per_device, 0).reshape(per_device, BLOCK, BLOCK).astype(jnp.float32)
        product = jnp.einsum("ekrc,ekcd->ekrd", couple, beside).astype(jnp.bfloat16)
        galerkin_terms = jnp.einsum("ecr,ekcd->ekrd", self_rows, product.astype(jnp.float32)).astype(jnp.bfloat16)
        rank_rows = lax.dynamic_slice_in_dim(owner_rank, (start * PAIRS).astype(jnp.int32), per_device * PAIRS, 0)
        block_rows = lax.dynamic_slice_in_dim(target_block, (start * PAIRS).astype(jnp.int32), per_device * PAIRS, 0)
        segment_keys = ((slab_index * domains + rank_rows) * CB_DEV + block_rows).astype(jnp.int32)
        coarse = coarse.at[segment_keys].add(galerkin_terms.reshape(per_device * PAIRS, square).astype(jnp.float32))
        return coarse, None

    coarse, unused = lax.scan(device_step, jnp.zeros((CB_TOTAL, square), jnp.float32), jnp.arange(slab_count * domains, dtype=jnp.int32))
    return coarse
```

```python
import functools

import jax
import jax.numpy as jnp
from jax import lax
from jax.experimental import pallas as pl
from jax.experimental.pallas import tpu as pltpu
from jax.sharding import PartitionSpec as P

BLOCK = 64
PAIRS = 7
EX = 8
EY = 4
EZ = 4
E_DEV = EX * EY * EZ
CB_DEV = 128
SQUARE = BLOCK * BLOCK
ROWS = SQUARE // 128
GROUP = 16
FACE = 32
ZERO_SLOT = E_DEV + 4 * FACE
DRAIN = 64


def spread_rows(flat, scratch, base):
    for t in range(ROWS):
        piece = flat(t).astype(jnp.float32)
        scratch[pl.ds(base + t, GROUP, stride=ROWS), :] = piece


def galerkin_kernel(
    rank_ref, block_ref, a_ref, p_ref, ym_ref, yp_ref, zm_ref, zp_ref, out_ref,
    acc, weights, lefts, rows, stage, sems,
):
    step = pl.program_id(0)
    low = lax.broadcasted_iota(jnp.int32, (ROWS, 128), 1) < BLOCK

    def both_orders(half_rows):
        return jnp.concatenate([half_rows, pltpu.roll(half_rows, BLOCK, 1)], axis=0)

    @pl.when(step == 0)
    def _prepare():
        def clear(i, _):
            acc[pl.ds(i * 8, 8)] = jnp.zeros((8, ROWS, 128), jnp.float32)
            return 0

        lax.fori_loop(0, acc.shape[0] // 8, clear, 0)
        weights[ZERO_SLOT] = jnp.zeros((128, 128), jnp.bfloat16)

        r = lax.broadcasted_iota(jnp.int32, (128, BLOCK), 0)
        c = lax.broadcasted_iota(jnp.int32, (128, BLOCK), 1)
        wanted = (((r % 2) + (r // BLOCK)) % 2) * ROWS + (r % BLOCK) // 2
        place = (c == wanted).astype(jnp.float32).astype(jnp.bfloat16)
        r = lax.broadcasted_iota(jnp.int32, (BLOCK, 128), 0)
        c = lax.broadcasted_iota(jnp.int32, (BLOCK, 128), 1)
        v = r // ROWS
        pick = (c == v * BLOCK + 2 * (r % ROWS) + v).astype(jnp.float32).astype(jnp.bfloat16)
        r = lax.broadcasted_iota(jnp.int32, (128, 128), 0)
        c = lax.broadcasted_iota(jnp.int32, (128, 128), 1)
        diagonal = (r // BLOCK) == (c // BLOCK)

        def prepare(ref, count, slot0, local):
            def group(g, _):
                base = pl.multiple_of(g * GROUP, GROUP)
                spread_rows(
                    lambda t: ref[pl.ds(base, GROUP), t * 128 : (t + 1) * 128], rows, 0
                )
                for i in range(GROUP):
                    own = rows[i * ROWS : (i + 1) * ROWS, :]
                    stacked = both_orders(own).astype(jnp.bfloat16)
                    wide = jnp.dot(place, stacked, preferred_element_type=jnp.float32)
                    wide = jnp.where(diagonal, wide, 0.0).astype(jnp.bfloat16)
                    weights[slot0 + base + i] = wide
                    if local:
                        left = lax.dot_general(
                            pick, stacked, (((1,), (1,)), ((), ())),
                            preferred_element_type=jnp.float32,
                        )
                        lefts[base + i] = left.astype(jnp.bfloat16)
                return 0

            lax.fori_loop(0, count // GROUP, group, 0)

        prepare(p_ref, E_DEV, 0, True)
        prepare(ym_ref, FACE, E_DEV, False)
        prepare(yp_ref, FACE, E_DEV + FACE, False)
        prepare(zm_ref, FACE, E_DEV + 2 * FACE, False)
        prepare(zp_ref, FACE, E_DEV + 3 * FACE, False)

    def relayout(k, _):
        spread_rows(
            lambda t: a_ref[k, :, t * 128 : (t + 1) * 128], rows, k * (GROUP * ROWS)
        )
        return 0

    lax.fori_loop(0, PAIRS, relayout, 0)

    def element(i, _):
        e = step * GROUP + i
        x = e % EX
        y = (e // EX) % EY
        z = e // (EX * EY)
        slots = (
            e,
            jnp.where(x > 0, e - 1, ZERO_SLOT),
            jnp.where(x < EX - 1, e + 1, ZERO_SLOT),
            jnp.where(y > 0, e - EX, E_DEV + z * EX + x),
            jnp.where(y < EY - 1, e + EX, E_DEV + FACE + z * EX + x),
            jnp.where(z > 0, e - EX * EY, E_DEV + 2 * FACE + y * EX + x),
            jnp.where(z < EZ - 1, e + EX * EY, E_DEV + 3 * FACE + y * EX + x),
        )
        stacked = []
        for k in range(PAIRS):
            start = pl.multiple_of((k * GROUP + i) * ROWS, ROWS)
            couple = rows[pl.ds(start, ROWS), :].astype(jnp.bfloat16)
            product = jnp.dot(couple, weights[slots[k]], preferred_element_type=jnp.float32)
            stacked.append(both_orders(product).astype(jnp.bfloat16))
        both = jnp.dot(
            lefts[e], jnp.concatenate(stacked, axis=1), preferred_element_type=jnp.float32
        )
        for k in range(PAIRS):
            own = both[:, k * 128 : (k + 1) * 128]
            term = jnp.where(low, own[:ROWS], own[ROWS:])
            target = rank_ref[e * PAIRS + k] * CB_DEV + block_ref[k, e]
            acc[target] += term.astype(jnp.bfloat16).astype(jnp.float32)
        return 0

    lax.fori_loop(0, GROUP, element, 0)

    @pl.when(step == pl.num_programs(0) - 1)
    def _drain():
        total = acc.shape[0] // DRAIN

        def copy(n, slot):
            return pltpu.make_async_copy(
                stage.at[slot], out_ref.at[pl.ds(n * DRAIN, DRAIN)], sems.at[slot]
            )

        def chunk(n, _):
            slot = n % 2

            @pl.when(n >= 2)
            def _():
                copy(n - 2, slot).wait()

            def cast(i, _):
                stage[slot, pl.ds(i * 8, 8)] = acc[pl.ds(n * DRAIN + i * 8, 8)].astype(
                    jnp.bfloat16
                )
                return 0

            lax.fori_loop(0, DRAIN // 8, cast, 0)
            copy(n, slot).start()
            return 0

        lax.fori_loop(0, total, chunk, 0)
        copy(total - 2, (total - 2) % 2).wait()
        copy(total - 1, (total - 1) % 2).wait()


def local_sums(ranks, blocks, a, p, halos, owners):
    whole = pl.BlockSpec(memory_space=pltpu.VMEM)
    smem = pl.BlockSpec(memory_space=pltpu.SMEM)
    return pl.pallas_call(
        galerkin_kernel,
        grid=(E_DEV // GROUP,),
        in_specs=[
            smem,
            smem,
            pl.BlockSpec((PAIRS, GROUP, SQUARE), lambda i: (0, i, 0)),
            whole, whole, whole, whole, whole,
        ],
        out_specs=pl.BlockSpec(memory_space=pl.ANY),
        out_shape=jax.ShapeDtypeStruct((owners * CB_DEV, ROWS, 128), jnp.bfloat16),
        scratch_shapes=[
            pltpu.VMEM((owners * CB_DEV, ROWS, 128), jnp.float32),
            pltpu.VMEM((ZERO_SLOT + 1, 128, 128), jnp.bfloat16),
            pltpu.VMEM((E_DEV, BLOCK, BLOCK), jnp.bfloat16),
            pltpu.VMEM((PAIRS * GROUP * ROWS, 128), jnp.float32),
            pltpu.VMEM((2, DRAIN, ROWS, 128), jnp.bfloat16),
            pltpu.SemaphoreType.DMA((2,)),
        ],
        compiler_params=pltpu.CompilerParams(
            dimension_semantics=("arbitrary",), vmem_limit_bytes=60 * 1024 * 1024
        ),
        name="galerkin_sums",
    )(ranks, blocks, a, p, *halos)


def faces(p):
    brick = p.reshape(EZ, EY, EX, SQUARE)
    found = []
    for axis, dim in (("dom", 1), ("slab", 0)):
        size = lax.axis_size(axis)
        up = [(i, i + 1) for i in range(size - 1)]
        down = [(j, i) for i, j in up]
        length = brick.shape[dim]
        last = lax.slice_in_dim(brick, length - 1, length, axis=dim).reshape(FACE, SQUARE)
        first = lax.slice_in_dim(brick, 0, 1, axis=dim).reshape(FACE, SQUARE)
        found += [lax.ppermute(last, axis, up), lax.ppermute(first, axis, down)]
    return found


def flat_kernel(in_ref, out_ref, scratch):
    scratch[...] = in_ref[...].reshape(GROUP * ROWS, 128).astype(jnp.float32)
    for t in range(ROWS):
        out_ref[:, t * 128 : (t + 1) * 128] = scratch[pl.ds(t, GROUP, stride=ROWS), :]


def flatten_blocks(x):
    return pl.pallas_call(
        flat_kernel,
        grid=(CB_DEV // GROUP,),
        in_specs=[pl.BlockSpec((GROUP, ROWS, 128), lambda i: (i, 0, 0))],
        out_specs=pl.BlockSpec((GROUP, SQUARE), lambda i: (i, 0)),
        out_shape=jax.ShapeDtypeStruct((CB_DEV, SQUARE), jnp.float32),
        scratch_shapes=[pltpu.VMEM((GROUP * ROWS, 128), jnp.float32)],
        name="flatten_blocks",
    )(x)


def on_device(a_blocks, p_blocks, dest_rank, dest_block):
    owners = lax.axis_size("dom")
    halos = faces(p_blocks)
    sums = local_sums(
        dest_rank.reshape(-1),
        dest_block.T,
        jnp.swapaxes(a_blocks, 0, 1),
        p_blocks,
        halos,
        owners,
    )
    mine = lax.psum_scatter(sums, "dom", scatter_dimension=0, tiled=True)
    return flatten_blocks(mine)


def solution(mesh):
    return jax.shard_map(
        on_device,
        mesh=mesh,
        in_specs=(
            P(("slab", "dom"), None, None),
            P(("slab", "dom"), None),
            P(("slab", "dom"), None),
            P(("slab", "dom"), None),
        ),
        out_specs=P(("slab", "dom"), None),
        check_vma=False,
    )
```

```python
import jax
import jax.numpy as jnp
from jax import lax
from jax.experimental import pallas as pl
from jax.experimental.pallas import tpu as pltpu
from jax.sharding import PartitionSpec as P

BLOCK = 64
PAIRS = 7
EX = 8
EY = 4
EZ = 4
E_DEV = EX * EY * EZ
CB_DEV = 128
SQUARE = BLOCK * BLOCK
ROWS = SQUARE // 128
HALF = ROWS // 2
GROUP = 16
FACE = 32
SIDE = 4
OWNERS = SIDE * SIDE
ZERO_SLOT = E_DEV + 4 * FACE
PART = CB_DEV // 4
SLOT = SIDE * PART
SLOTS = OWNERS * CB_DEV // SLOT
BUFFERS = 4
SLOT_OF = 0x53201476


def spread_rows(flat, scratch, base):
    for t in range(ROWS):
        scratch[pl.ds(base + t, GROUP, stride=ROWS), :] = flat(t).astype(jnp.float32)


def clear(acc):
    def body(i, _):
        acc[pl.ds(i * 16, 16)] = jnp.zeros((16, HALF, 128), jnp.float32)
        return 0

    lax.fori_loop(0, acc.shape[0] // 16, body, 0)


def add_terms(step, half, target_ref, lefts, q_ref, acc):
    low = lax.broadcasted_iota(jnp.int32, (HALF, PAIRS * 128), 1) % 128 < BLOCK

    def element(i, _):
        e = step * GROUP + i
        both = jnp.dot(
            lefts[e, half * ROWS : (half + 1) * ROWS, :], q_ref[i],
            preferred_element_type=jnp.float32,
        )
        terms = jnp.where(low, both[:HALF], both[HALF:])
        terms = terms.astype(jnp.bfloat16).astype(jnp.float32)
        for k in range(PAIRS):
            acc[target_ref[e * PAIRS + k]] += terms[:, k * 128 : (k + 1) * 128]
        return 0

    lax.fori_loop(0, GROUP, element, 0, unroll=4)


def drain(acc, stage, sems, outs):
    places = []
    for out in outs:
        places += [out.at[i] for i in range(out.shape[0])]
    copies = []
    for n in range(SLOTS):
        buffer = n % BUFFERS
        if n >= BUFFERS:
            copies[n - BUFFERS].wait()

        def cast(i, _):
            blocks = acc[pl.ds(n * SLOT + i * 16, 16)]
            stage[buffer, pl.ds(i * 16, 16)] = blocks.astype(jnp.bfloat16)
            return 0

        lax.fori_loop(0, SLOT // 16, cast, 0)
        copy = pltpu.make_async_copy(stage.at[buffer], places[n], sems.at[buffer])
        copy.start()
        copies.append(copy)
    for copy in copies[-BUFFERS:]:
        copy.wait()


def first_kernel(target_ref, a_ref, p_ref, ym_ref, yp_ref, zm_ref, zp_ref, *refs):
    q_ref, left_ref, *outs = refs[:12]
    acc, weights, rows, stage, sems = refs[12:]
    step = pl.program_id(0)

    @pl.when(step == 0)
    def _prepare():
        clear(acc)
        weights[ZERO_SLOT] = jnp.zeros((128, 256), jnp.bfloat16)
        low = lax.broadcasted_iota(jnp.int32, (ROWS, 128), 1) < BLOCK
        low2 = lax.broadcasted_iota(jnp.int32, (BLOCK, 128), 1) < BLOCK
        r = lax.broadcasted_iota(jnp.int32, (BLOCK, BLOCK), 0)
        c = lax.broadcasted_iota(jnp.int32, (BLOCK, BLOCK), 1)
        place = (c == (r % 2) * ROWS + r // 2).astype(jnp.float32).astype(jnp.bfloat16)
        r = lax.broadcasted_iota(jnp.int32, (BLOCK, 128), 0)
        c = lax.broadcasted_iota(jnp.int32, (BLOCK, 128), 1)
        v = (r // HALF) % 2
        lane = v * BLOCK + 2 * ((r // ROWS) * HALF + r % HALF) + v
        pick = (c == lane).astype(jnp.float32).astype(jnp.bfloat16)

        def prepare(ref, count, slot0, local):
            def group(g, _):
                base = pl.multiple_of(g * GROUP, GROUP)
                spread_rows(
                    lambda t: ref[pl.ds(base, GROUP), t * 128 : (t + 1) * 128], rows, 0
                )
                for i in range(0, GROUP, 2):
                    ordered = []
                    for j in (i, i + 1):
                        own = rows[j * ROWS : (j + 1) * ROWS, :]
                        turned = pltpu.roll(own, BLOCK, 1)
                        ordered.append(
                            jnp.concatenate(
                                [jnp.where(low, own, turned), jnp.where(low, turned, own)], axis=0
                            ).astype(jnp.bfloat16)
                        )
                        if local:
                            stacked = jnp.concatenate([own, turned], axis=0)
                            left = lax.dot_general(
                                pick, stacked.astype(jnp.bfloat16), (((1,), (1,)), ((), ())),
                                preferred_element_type=jnp.float32,
                            )
                            left_ref[base + j] = left.astype(jnp.bfloat16)
                    placed = jnp.dot(
                        place, jnp.concatenate(ordered, axis=1), preferred_element_type=jnp.float32
                    )
                    for j in (0, 1):
                        twice = placed[:, j * 128 : (j + 1) * 128]
                        at_low = jnp.where(low2, twice, 0.0).astype(jnp.bfloat16)
                        at_high = jnp.where(low2, 0.0, twice).astype(jnp.bfloat16)
                        slot = slot0 + base + i + j
                        weights[slot, :BLOCK, :128] = at_low
                        weights[slot, :BLOCK, 128:] = at_high
                        weights[slot, BLOCK:, :128] = at_high
                        weights[slot, BLOCK:, 128:] = at_low
                return 0

            lax.fori_loop(0, count // GROUP, group, 0)

        prepare(p_ref, E_DEV, 0, True)
        prepare(ym_ref, FACE, E_DEV, False)
        prepare(yp_ref, FACE, E_DEV + FACE, False)
        prepare(zm_ref, FACE, E_DEV + 2 * FACE, False)
        prepare(zp_ref, FACE, E_DEV + 3 * FACE, False)

    for k in range(PAIRS):
        spread_rows(
            lambda t: a_ref[k, :, t * 128 : (t + 1) * 128], rows, k * (GROUP * ROWS)
        )

    def element(i, _):
        e = step * GROUP + i
        x = e % EX
        y = (e // EX) % EY
        z = e // (EX * EY)
        slots = (
            e,
            jnp.where(x > 0, e - 1, ZERO_SLOT),
            jnp.where(x < EX - 1, e + 1, ZERO_SLOT),
            jnp.where(y > 0, e - EX, E_DEV + z * EX + x),
            jnp.where(y < EY - 1, e + EX, E_DEV + FACE + z * EX + x),
            jnp.where(z > 0, e - EX * EY, E_DEV + 2 * FACE + y * EX + x),
            jnp.where(z < EZ - 1, e + EX * EY, E_DEV + 3 * FACE + y * EX + x),
        )
        for k in range(PAIRS):
            start = pl.multiple_of((k * GROUP + i) * ROWS, ROWS)
            couple = rows[pl.ds(start, ROWS), :].astype(jnp.bfloat16)
            product = jnp.dot(couple, weights[slots[k]], preferred_element_type=jnp.float32)
            product = product.astype(jnp.bfloat16)
            q_ref[i, :ROWS, k * 128 : (k + 1) * 128] = product[:, :128]
            q_ref[i, ROWS:, k * 128 : (k + 1) * 128] = product[:, 128:]
        return 0

    lax.fori_loop(0, GROUP, element, 0, unroll=4)
    add_terms(step, 0, target_ref, left_ref, q_ref, acc)

    @pl.when(step == pl.num_programs(0) - 1)
    def _drain():
        drain(acc, stage, sems, outs)


def second_kernel(target_ref, left_ref, q_ref, *refs):
    outs = refs[:10]
    acc, stage, sems = refs[10:]
    step = pl.program_id(0)

    @pl.when(step == 0)
    def _clear():
        clear(acc)

    add_terms(step, 1, target_ref, left_ref, q_ref, acc)

    @pl.when(step == pl.num_programs(0) - 1)
    def _drain():
        drain(acc, stage, sems, outs)


VMEM = pl.BlockSpec(memory_space=pltpu.VMEM)
SMEM = pl.BlockSpec(memory_space=pltpu.SMEM)
HBM = pl.BlockSpec(memory_space=pl.ANY)
Q_SPEC = pl.BlockSpec((GROUP, BLOCK, PAIRS * 128), lambda i: (i, 0, 0))
PACKS = [
    jax.ShapeDtypeStruct((n, SLOT, HALF, 128), jnp.bfloat16) for n in (2, 2, 1, 1, 2) * 2
]
SUMS = [
    pltpu.VMEM((BUFFERS, SLOT, HALF, 128), jnp.bfloat16),
    pltpu.SemaphoreType.DMA((BUFFERS,)),
]


def params():
    return pltpu.CompilerParams(
        dimension_semantics=("arbitrary",), vmem_limit_bytes=56 * 1024 * 1024
    )


def first_half(target, a, p, halos):
    found = pl.pallas_call(
        first_kernel,
        grid=(E_DEV // GROUP,),
        in_specs=[
            SMEM,
            pl.BlockSpec((PAIRS, GROUP, SQUARE), lambda i: (0, i, 0)),
            VMEM, VMEM, VMEM, VMEM, VMEM,
        ],
        out_specs=[Q_SPEC, VMEM] + [HBM] * len(PACKS),
        out_shape=[
            jax.ShapeDtypeStruct((E_DEV, BLOCK, PAIRS * 128), jnp.bfloat16),
            jax.ShapeDtypeStruct((E_DEV, BLOCK, BLOCK), jnp.bfloat16),
        ]
        + PACKS,
        scratch_shapes=[
            pltpu.VMEM((OWNERS * CB_DEV, HALF, 128), jnp.float32),
            pltpu.VMEM((ZERO_SLOT + 1, 128, 256), jnp.bfloat16),
            pltpu.VMEM((PAIRS * GROUP * ROWS, 128), jnp.float32),
        ]
        + SUMS,
        compiler_params=params(),
        cost_estimate=pl.CostEstimate(
            flops=10**10, bytes_accessed=40 * 10**6, transcendentals=0
        ),
        name="first_half",
    )(target, a, p, *halos)
    return found[0], found[1], found[2:]


def second_half(target, lefts, q):
    return pl.pallas_call(
        second_kernel,
        grid=(E_DEV // GROUP,),
        in_specs=[SMEM, VMEM, Q_SPEC],
        out_specs=[HBM] * len(PACKS),
        out_shape=PACKS,
        scratch_shapes=[pltpu.VMEM((OWNERS * CB_DEV, HALF, 128), jnp.float32)] + SUMS,
        compiler_params=params(),
        cost_estimate=pl.CostEstimate(
            flops=10**10, bytes_accessed=40 * 10**6, transcendentals=0
        ),
        name="second_half",
    )(target, lefts, q)


def faces(p):
    brick = p.reshape(EZ, EY, EX, SQUARE)
    found = []
    for axis, dim in (("dom", 1), ("slab", 0)):
        size = lax.axis_size(axis)
        up = [(i, i + 1) for i in range(size - 1)]
        down = [(j, i) for i, j in up]
        length = brick.shape[dim]
        last = lax.slice_in_dim(brick, length - 1, length, axis=dim).reshape(FACE, SQUARE)
        first = lax.slice_in_dim(brick, 0, 1, axis=dim).reshape(FACE, SQUARE)
        found += [lax.ppermute(last, axis, up), lax.ppermute(first, axis, down)]
    return found


def sum_places(dest_rank, dest_block):
    me = lax.axis_index("dom")
    rank = dest_rank.reshape(-1)
    block = dest_block.reshape(-1)
    dx = (rank - me) % SIDE
    dy = (rank // SIDE - me // SIDE) % SIDE
    which = block // (2 * PART)
    part = (block // PART) % 2
    hops = jnp.where(which == 0, dx, dy)
    other = jnp.where(which == 0, dy, dx)
    slot = (SLOT_OF >> (4 * (2 * hops + part))) & 7
    return ((which * (SLOTS // 2) + slot) * SIDE + other) * PART + block % PART


def ring_perms():
    def moved(dx, dy):
        return [
            (y * SIDE + x, (y + dy) % SIDE * SIDE + (x + dx) % SIDE)
            for y in range(SIDE)
            for x in range(SIDE)
        ]

    return (moved(1, 0), moved(-1, 0)), (moved(0, 1), moved(0, -1))


def added(*parts):
    total = parts[0].astype(jnp.float32)
    for part in parts[1:]:
        total = total + part.astype(jnp.float32)
    return total


def ring_sum(right, left, keep_right, keep_left, own, perms):
    forward, backward = perms
    r1 = lax.ppermute(right, "dom", forward)
    l1 = lax.ppermute(left, "dom", backward)
    r2 = lax.ppermute(added(keep_right, r1[0]).astype(jnp.bfloat16), "dom", forward)
    l2 = lax.ppermute(added(keep_left, l1[0]).astype(jnp.bfloat16), "dom", backward)
    return (own[0], r2, l1[1]), (own[1], r1[1], l2)


def exchange(packs):
    along_x, along_y = ring_perms()
    found = []
    for which, (one, two) in enumerate(((along_x, along_y), (along_y, along_x))):
        right, left, keep_right, keep_left, own = packs[which * 5 : which * 5 + 5]
        first = ring_sum(right, left, keep_right[0], keep_left[0], own, one)
        r, l = (added(*parts).reshape(SIDE, PART, HALF, 128) for parts in first)
        rb, lb = r.astype(jnp.bfloat16), l.astype(jnp.bfloat16)
        found += ring_sum(
            jnp.stack([rb[2], lb[1]]), jnp.stack([lb[2], rb[3]]), rb[1], lb[3], (r[0], l[0]), two
        )
    return found


def finish_kernel(*refs):
    *ins, out_ref, scratch = refs
    for n in range(len(ins) // 3):
        total = ins[3 * n][...] + ins[3 * n + 1][...].astype(jnp.float32)
        total = total + ins[3 * n + 2][...].astype(jnp.float32)
        half, part = divmod(n, 4)
        scratch[...] = total.reshape(PART * HALF, 128)
        for u in range(HALF):
            t = half * HALF + u
            out_ref[part * PART : (part + 1) * PART, t * 128 : (t + 1) * 128] = scratch[
                pl.ds(u, PART, stride=HALF), :
            ]


def finish(parts):
    flat = [array for triple in parts for array in triple]
    return pl.pallas_call(
        finish_kernel,
        in_specs=[VMEM] * len(flat),
        out_specs=VMEM,
        out_shape=jax.ShapeDtypeStruct((CB_DEV, SQUARE), jnp.float32),
        scratch_shapes=[pltpu.VMEM((PART * HALF, 128), jnp.float32)],
        name="finish",
    )(*flat)


def on_device(a_blocks, p_blocks, dest_rank, dest_block):
    halos = faces(p_blocks)
    target = sum_places(dest_rank, dest_block)
    q, lefts, packs = first_half(target, jnp.swapaxes(a_blocks, 0, 1), p_blocks, halos)
    parts = exchange(packs)
    parts += exchange(second_half(target, lefts, q))
    return finish(parts)


def solution(mesh):
    return jax.shard_map(
        on_device,
        mesh=mesh,
        in_specs=(
            P(("slab", "dom"), None, None),
            P(("slab", "dom"), None),
            P(("slab", "dom"), None),
            P(("slab", "dom"), None),
        ),
        out_specs=P(("slab", "dom"), None),
        check_vma=False,
    )
```

```python
import jax
import jax.numpy as jnp
from jax import lax
from jax.experimental import pallas as pl
from jax.experimental.pallas import tpu as pltpu
from jax.sharding import PartitionSpec as P

BLOCK = 64
PAIRS = 7
EX = 8
EY = 4
EZ = 4
E_DEV = EX * EY * EZ
CB_DEV = 128
SQUARE = BLOCK * BLOCK
ROWS = SQUARE // 128
HALF = ROWS // 2
PITCH = 33
FLAT_PITCH = 17
GROUP = 16
FACE = 32
SIDE = 4
OWNERS = SIDE * SIDE
PART = CB_DEV // 4
SLOT = SIDE * PART
SLOTS = OWNERS * CB_DEV // SLOT
BUFFERS = 4
SLOT_OF = 0x53201476


def spread_rows(flat, scratch, base):
    for t in range(ROWS):
        scratch[pl.ds(base + t, GROUP, stride=PITCH), :] = flat(t).astype(jnp.float32)


def piece(scratch, index):
    return scratch[pl.ds(index * PITCH, ROWS), :]


def clear(acc):
    def body(i, _):
        acc[pl.ds(i * 16, 16)] = jnp.zeros((16, HALF, 128), jnp.float32)
        return 0

    lax.fori_loop(0, OWNERS * CB_DEV // 16, body, 0)


def spread_weights(ref, base, rows, weights, slot0, lefts):
    low = lax.broadcasted_iota(jnp.int32, (ROWS, 128), 1) < BLOCK
    low2 = lax.broadcasted_iota(jnp.int32, (BLOCK, 128), 1) < BLOCK
    r = lax.broadcasted_iota(jnp.int32, (BLOCK, BLOCK), 0)
    c = lax.broadcasted_iota(jnp.int32, (BLOCK, BLOCK), 1)
    place = (c == (r % 2) * ROWS + r // 2).astype(jnp.float32).astype(jnp.bfloat16)
    r = lax.broadcasted_iota(jnp.int32, (BLOCK, 128), 0)
    c = lax.broadcasted_iota(jnp.int32, (BLOCK, 128), 1)
    v = (r // HALF) % 2
    lane = v * BLOCK + 2 * ((r // ROWS) * HALF + r % HALF) + v
    pick = (c == lane).astype(jnp.float32).astype(jnp.bfloat16)
    spread_rows(lambda t: ref[pl.ds(base, GROUP), t * 128 : (t + 1) * 128], rows, 0)
    for i in range(0, GROUP, 2):
        ordered = []
        for j in (i, i + 1):
            own = piece(rows, j)
            turned = pltpu.roll(own, BLOCK, 1)
            ordered.append(
                jnp.concatenate(
                    [jnp.where(low, own, turned), jnp.where(low, turned, own)], axis=0
                ).astype(jnp.bfloat16)
            )
            if lefts is not None:
                stacked = jnp.concatenate([own, turned], axis=0)
                left = lax.dot_general(
                    pick, stacked.astype(jnp.bfloat16), (((1,), (1,)), ((), ())),
                    preferred_element_type=jnp.float32,
                )
                lefts[base + j] = left.astype(jnp.bfloat16)
        placed = jnp.dot(
            place, jnp.concatenate(ordered, axis=1), preferred_element_type=jnp.float32
        )
        for j in (0, 1):
            twice = placed[:, j * 128 : (j + 1) * 128]
            at_low = jnp.where(low2, twice, 0.0).astype(jnp.bfloat16)
            at_high = jnp.where(low2, 0.0, twice).astype(jnp.bfloat16)
            weights[slot0 + i + j, :BLOCK, :128] = at_low
            weights[slot0 + i + j, :BLOCK, 128:] = at_high
            weights[slot0 + i + j, BLOCK:, :128] = at_high
            weights[slot0 + i + j, BLOCK:, 128:] = at_low


def product_kernel(a_ref, p_ref, q_out, left_ref, face_ref, couples, q, rows, weights, sems):
    step = pl.program_id(0)
    start = pl.multiple_of(step * GROUP, GROUP)
    spread_weights(p_ref, start, rows, weights, start, left_ref)
    for k in range(PAIRS):
        spread_rows(
            lambda t: a_ref[k, :, t * 128 : (t + 1) * 128], rows, k * (GROUP * PITCH)
        )

    def lay(i, _):
        for k in range(PAIRS):
            couples[k, step * GROUP + i] = piece(rows, k * GROUP + i).astype(jnp.bfloat16)
        return 0

    lax.fori_loop(0, GROUP, lay, 0, unroll=4)

    @pl.when(step == pl.num_programs(0) - 1)
    def _multiply():
        plane = EX * EY

        def copy(n):
            span = pl.ds(n * GROUP, GROUP)
            return pltpu.make_async_copy(q.at[span], q_out.at[span], sems.at[n])

        behind = plane // GROUP

        for z in range(EZ):
            for g in range(plane // GROUP):
                base = z * plane + g * GROUP
                def neighbour(i, _):
                    j = base + i
                    x = j % EX
                    y = (j // EX) % EY
                    inside = (
                        None, x < EX - 1, x > 0, y < EY - 1, y > 0,
                        z < EZ - 1 or None, z > 0 or None,
                    )
                    away = (0, 1, -1, EX, -EX, plane, -plane)
                    here = [k for k in range(PAIRS) if k < 5 or inside[k]]
                    owners = [
                        j + away[k] if inside[k] is None or k >= 5
                        else jnp.where(inside[k], j + away[k], E_DEV)
                        for k in here
                    ]
                    left = jnp.concatenate(
                        [couples[k, e] for k, e in zip(here, owners)], axis=0
                    )
                    found = jnp.dot(left, weights[j], preferred_element_type=jnp.float32)
                    found = found.astype(jnp.bfloat16)
                    for n, (k, e) in enumerate(zip(here, owners)):
                        own = found[n * ROWS : (n + 1) * ROWS]
                        q[e, :ROWS, k * 128 : (k + 1) * 128] = own[:, :128]
                        q[e, ROWS:, k * 128 : (k + 1) * 128] = own[:, 128:]
                    return 0

                lax.fori_loop(0, GROUP, neighbour, 0, unroll=4)
                if base // GROUP >= behind:
                    copy(base // GROUP - behind).start()
        for n in range(E_DEV // GROUP - behind, E_DEV // GROUP):
            copy(n).start()
        for n in range(FACE):
            outer, x = divmod(n, EX)
            face_ref[n] = couples[3, outer * plane + x]
            face_ref[FACE + n] = couples[4, outer * plane + plane - EX + x]
            face_ref[2 * FACE + n] = couples[5, n]
            face_ref[3 * FACE + n] = couples[6, E_DEV - plane + n]
        for n in range(E_DEV // GROUP):
            copy(n).wait()


def add_terms(step, half, target_ref, lefts, q_ref, acc):
    low = lax.broadcasted_iota(jnp.int32, (HALF, PAIRS * 128), 1) % 128 < BLOCK

    def element(i, _):
        e = step * GROUP + i
        x = e % EX
        y = (e // EX) % EY
        z = e // (EX * EY)
        inside = (None, x > 0, x < EX - 1, y > 0, y < EY - 1, z > 0, z < EZ - 1)
        both = jnp.dot(
            lefts[e, half * ROWS : (half + 1) * ROWS, :], q_ref[i],
            preferred_element_type=jnp.float32,
        )
        terms = jnp.where(low, both[:HALF], both[HALF:])
        terms = terms.astype(jnp.bfloat16).astype(jnp.float32)
        for k in range(PAIRS):
            target = target_ref[e * PAIRS + k]
            if inside[k] is not None:
                target = jnp.where(inside[k], target, OWNERS * CB_DEV)
            acc[target] += terms[:, k * 128 : (k + 1) * 128]
        return 0

    lax.fori_loop(0, GROUP, element, 0, unroll=4)


def add_face_terms(step, half, target_ref, lefts, qh_ref, acc):
    low = lax.broadcasted_iota(jnp.int32, (HALF, 128), 1) < BLOCK
    plane = EX * EY
    face = step // (FACE // GROUP)

    def pair(i, _):
        n = step % (FACE // GROUP) * GROUP + i
        column = n // EX * plane + n % EX
        e = jnp.where(
            face < 2, column + face * (plane - EX), n + (face - 2) * (E_DEV - plane)
        )
        both = jnp.dot(
            lefts[e, half * ROWS : (half + 1) * ROWS, :], qh_ref[step * GROUP + i],
            preferred_element_type=jnp.float32,
        )
        term = jnp.where(low, both[:HALF], both[HALF:])
        acc[target_ref[e * PAIRS + 3 + face]] += term.astype(jnp.bfloat16).astype(jnp.float32)
        return 0

    lax.fori_loop(0, GROUP, pair, 0, unroll=8)


def drain(acc, stage, sems, outs):
    places = []
    for out in outs:
        places += [out.at[i] for i in range(out.shape[0])]
    copies = []
    for n in range(SLOTS):
        buffer = n % BUFFERS
        if n >= BUFFERS:
            copies[n - BUFFERS].wait()

        def cast(i, _):
            blocks = acc[pl.ds(n * SLOT + i * 16, 16)]
            stage[buffer, pl.ds(i * 16, 16)] = blocks.astype(jnp.bfloat16)
            return 0

        lax.fori_loop(0, SLOT // 16, cast, 0)
        copy = pltpu.make_async_copy(stage.at[buffer], places[n], sems.at[buffer])
        copy.start()
        copies.append(copy)
    for copy in copies[-BUFFERS:]:
        copy.wait()


def first_kernel(target_ref, left_ref, q_ref, face_ref, ym_ref, yp_ref, zm_ref, zp_ref, *refs):
    qh_ref, *outs = refs[:11]
    acc, stage, sems, weights, rows = refs[11:]
    step = pl.program_id(0)

    @pl.when(step == 0)
    def _clear():
        clear(acc)

    groups = FACE // GROUP
    for f, ref in enumerate((ym_ref, yp_ref, zm_ref, zp_ref)):

        @pl.when(step // groups == f)
        def _weights():
            base = pl.multiple_of(step % groups * GROUP, GROUP)
            spread_weights(ref, base, rows, weights, 0, None)

    def multiply(i, _):
        n = step * GROUP + i
        found = jnp.dot(face_ref[n], weights[i], preferred_element_type=jnp.float32)
        found = found.astype(jnp.bfloat16)
        qh_ref[n, :ROWS, :] = found[:, :128]
        qh_ref[n, ROWS:, :] = found[:, 128:]
        return 0

    lax.fori_loop(0, GROUP, multiply, 0, unroll=8)
    add_face_terms(step, 0, target_ref, left_ref, qh_ref, acc)
    add_terms(step, 0, target_ref, left_ref, q_ref, acc)

    @pl.when(step == pl.num_programs(0) - 1)
    def _drain():
        drain(acc, stage, sems, outs)


def second_kernel(target_ref, left_ref, q_ref, qh_ref, *refs):
    outs = refs[:10]
    acc, stage, sems = refs[10:]
    step = pl.program_id(0)

    @pl.when(step == 0)
    def _clear():
        clear(acc)

    add_face_terms(step, 1, target_ref, left_ref, qh_ref, acc)
    add_terms(step, 1, target_ref, left_ref, q_ref, acc)

    @pl.when(step == pl.num_programs(0) - 1)
    def _drain():
        drain(acc, stage, sems, outs)


VMEM = pl.BlockSpec(memory_space=pltpu.VMEM)
SMEM = pl.BlockSpec(memory_space=pltpu.SMEM)
HBM = pl.BlockSpec(memory_space=pl.ANY)
Q_SPEC = pl.BlockSpec((GROUP, BLOCK, PAIRS * 128), lambda i: (i, 0, 0))
PACKS = [
    jax.ShapeDtypeStruct((n, SLOT, HALF, 128), jnp.bfloat16) for n in (2, 2, 1, 1, 2) * 2
]
SUMS = [
    pltpu.VMEM((OWNERS * CB_DEV + 1, HALF, 128), jnp.float32),
    pltpu.VMEM((BUFFERS, SLOT, HALF, 128), jnp.bfloat16),
    pltpu.SemaphoreType.DMA((BUFFERS,)),
]
WEIGHTS = pltpu.VMEM((GROUP, 128, 256), jnp.bfloat16)


def params():
    return pltpu.CompilerParams(
        dimension_semantics=("arbitrary",), vmem_limit_bytes=48 * 1024 * 1024
    )


def cost(megabytes):
    return pl.CostEstimate(flops=10**10, bytes_accessed=megabytes * 10**6, transcendentals=0)


def local_products(a, p):
    return pl.pallas_call(
        product_kernel,
        grid=(E_DEV // GROUP,),
        in_specs=[pl.BlockSpec((PAIRS, GROUP, SQUARE), lambda i: (0, i, 0)), VMEM],
        out_specs=[HBM, VMEM, VMEM],
        out_shape=[
            jax.ShapeDtypeStruct((E_DEV, BLOCK, PAIRS * 128), jnp.bfloat16),
            jax.ShapeDtypeStruct((E_DEV, BLOCK, BLOCK), jnp.bfloat16),
            jax.ShapeDtypeStruct((4 * FACE, ROWS, 128), jnp.bfloat16),
        ],
        scratch_shapes=[
            pltpu.VMEM((PAIRS, E_DEV + 1, ROWS, 128), jnp.bfloat16),
            pltpu.VMEM((E_DEV + 1, BLOCK, PAIRS * 128), jnp.bfloat16),
            pltpu.VMEM((PAIRS * GROUP * PITCH + 8, 128), jnp.float32),
            pltpu.VMEM((E_DEV, 128, 256), jnp.bfloat16),
            pltpu.SemaphoreType.DMA((E_DEV // GROUP,)),
        ],
        compiler_params=params(),
        cost_estimate=cost(60),
        name="local_products",
    )(a, p)


def first_half(target, lefts, q, face, halos):
    found = pl.pallas_call(
        first_kernel,
        grid=(E_DEV // GROUP,),
        in_specs=[SMEM, VMEM, Q_SPEC, VMEM, VMEM, VMEM, VMEM, VMEM],
        out_specs=[VMEM] + [HBM] * len(PACKS),
        out_shape=[jax.ShapeDtypeStruct((4 * FACE, BLOCK, 128), jnp.bfloat16)] + PACKS,
        scratch_shapes=SUMS + [WEIGHTS, pltpu.VMEM((GROUP * PITCH + 8, 128), jnp.float32)],
        compiler_params=params(),
        cost_estimate=cost(60),
        name="first_half",
    )(target, lefts, q, face, *halos)
    return found[0], found[1:]


def second_half(target, lefts, q, qh):
    return pl.pallas_call(
        second_kernel,
        grid=(E_DEV // GROUP,),
        in_specs=[SMEM, VMEM, Q_SPEC, VMEM],
        out_specs=[HBM] * len(PACKS),
        out_shape=PACKS,
        scratch_shapes=SUMS,
        compiler_params=params(),
        cost_estimate=cost(60),
        name="second_half",
    )(target, lefts, q, qh)


def faces(p):
    brick = p.reshape(EZ, EY, EX, SQUARE)
    found = []
    for axis, dim in (("dom", 1), ("slab", 0)):
        size = lax.axis_size(axis)
        up = [(i, i + 1) for i in range(size - 1)]
        down = [(j, i) for i, j in up]
        length = brick.shape[dim]
        last = lax.slice_in_dim(brick, length - 1, length, axis=dim).reshape(FACE, SQUARE)
        first = lax.slice_in_dim(brick, 0, 1, axis=dim).reshape(FACE, SQUARE)
        found += [lax.ppermute(last, axis, up), lax.ppermute(first, axis, down)]
    return found


def sum_places(dest_rank, dest_block):
    me = lax.axis_index("dom")
    rank = dest_rank.reshape(-1)
    block = dest_block.reshape(-1)
    dx = (rank - me) % SIDE
    dy = (rank // SIDE - me // SIDE) % SIDE
    which = block // (2 * PART)
    part = (block // PART) % 2
    hops = jnp.where(which == 0, dx, dy)
    other = jnp.where(which == 0, dy, dx)
    slot = (SLOT_OF >> (4 * (2 * hops + part))) & 7
    return ((which * (SLOTS // 2) + slot) * SIDE + other) * PART + block % PART


def ring_perms():
    def moved(dx, dy):
        return [
            (y * SIDE + x, (y + dy) % SIDE * SIDE + (x + dx) % SIDE)
            for y in range(SIDE)
            for x in range(SIDE)
        ]

    return (moved(1, 0), moved(-1, 0)), (moved(0, 1), moved(0, -1))


def added(*parts):
    total = parts[0].astype(jnp.float32)
    for part in parts[1:]:
        total = total + part.astype(jnp.float32)
    return total


def join(keep, arrived):
    return added(keep, arrived).astype(jnp.bfloat16)


def sum_of_rows(packs, perms):
    right, left, keep_right, keep_left, own = packs
    forward, backward = perms
    r1 = lax.ppermute(right, "dom", forward)
    l1 = lax.ppermute(left, "dom", backward)
    r2 = lax.ppermute(join(keep_right[0], r1[0]), "dom", forward)
    l2 = lax.ppermute(join(keep_left[0], l1[0]), "dom", backward)
    shape = (SIDE, PART, HALF, 128)
    return added(own[0], r2, l1[1]).reshape(shape), added(own[1], r1[1], l2).reshape(shape)


def exchange(halves):
    along_x, along_y = ring_perms()
    found = []
    for which, (one, two) in enumerate(((along_x, along_y), (along_y, along_x))):
        sums = [sum_of_rows(packs[which * 5 : which * 5 + 5], one) for packs in halves]
        r = [jnp.stack([s[0][n] for s in sums]) for n in range(3)]
        l = [jnp.stack([s[1][n] for s in sums]) for n in (0, 1, 2, 3)]
        r16 = [v.astype(jnp.bfloat16) for v in r]
        l16 = [v.astype(jnp.bfloat16) for v in l]
        r3 = jnp.stack([s[0][3] for s in sums]).astype(jnp.bfloat16)
        forward, backward = two
        r1 = lax.ppermute(jnp.stack([r16[2], l16[1]]), "dom", forward)
        l1 = lax.ppermute(jnp.stack([l16[2], r3]), "dom", backward)
        r2 = lax.ppermute(join(r16[1], r1[0]), "dom", forward)
        l2 = lax.ppermute(join(l16[3], l1[0]), "dom", backward)
        found += [r[0], l[0], r1, l1, r2, l2]
    return found


def finish_kernel(*refs):
    *ins, out_ref, scratch = refs
    for which in range(2):
        own_right, own_left, r1, l1, r2, l2 = ins[6 * which : 6 * which + 6]
        for half in range(2):
            parts = (
                (own_right[half], r2[half], l1[1, half]),
                (own_left[half], r1[1, half], l2[half]),
            )
            for part, pieces in enumerate(parts):
                total = added(*pieces)
                for c in range(PART):
                    scratch[c * FLAT_PITCH : c * FLAT_PITCH + HALF, :] = total[c]
                rows = pl.ds((2 * which + part) * PART, PART)
                for u in range(HALF):
                    t = half * HALF + u
                    out_ref[rows, t * 128 : (t + 1) * 128] = scratch[
                        pl.ds(u, PART, stride=FLAT_PITCH), :
                    ]


def finish(parts):
    return pl.pallas_call(
        finish_kernel,
        in_specs=[VMEM] * len(parts),
        out_specs=VMEM,
        out_shape=jax.ShapeDtypeStruct((CB_DEV, SQUARE), jnp.float32),
        scratch_shapes=[pltpu.VMEM((PART * FLAT_PITCH + 8, 128), jnp.float32)],
        name="finish",
    )(*parts)


def on_device(a_blocks, p_blocks, dest_rank, dest_block):
    halos = faces(p_blocks)
    target = sum_places(dest_rank, dest_block)
    q, lefts, face = local_products(jnp.swapaxes(a_blocks, 0, 1), p_blocks)
    qh, first = first_half(target, lefts, q, face, halos)
    second = second_half(target, lefts, q, qh)
    return finish(exchange((first, second)))


def solution(mesh):
    return jax.shard_map(
        on_device,
        mesh=mesh,
        in_specs=(
            P(("slab", "dom"), None, None),
            P(("slab", "dom"), None),
            P(("slab", "dom"), None),
            P(("slab", "dom"), None),
        ),
        out_specs=P(("slab", "dom"), None),
        check_vma=False,
    )
```

```python
import jax
import jax.numpy as jnp
from jax import lax
from jax.experimental import pallas as pl
from jax.experimental.pallas import tpu as pltpu
from jax.sharding import PartitionSpec as P

BLOCK = 64
PAIRS = 7
EX = 8
EY = 4
EZ = 4
E_DEV = EX * EY * EZ
CB_DEV = 128
SQUARE = BLOCK * BLOCK
ROWS = SQUARE // 128
HALF = ROWS // 2
PITCH = 33
FLAT_PITCH = 17
GROUP = 16
FACE = 32
SIDE = 4
OWNERS = SIDE * SIDE
PART = CB_DEV // 4
SLOT = SIDE * PART
SLOTS = OWNERS * CB_DEV // SLOT
BUFFERS = 4
SLOT_OF = 0x53201476


def spread_rows(flat, scratch, base):
    for t in range(ROWS):
        scratch[pl.ds(base + t, GROUP, stride=PITCH), :] = flat(t).astype(jnp.float32)


def piece(scratch, index):
    return scratch[pl.ds(index * PITCH, ROWS), :]


def clear(acc):
    def body(i, _):
        acc[pl.ds(i * 16, 16)] = jnp.zeros((16, HALF, 128), jnp.float32)
        return 0

    lax.fori_loop(0, OWNERS * CB_DEV // 16, body, 0)


def spread_weights(ref, base, rows, weights, slot0, lefts):
    low = lax.broadcasted_iota(jnp.int32, (ROWS, 128), 1) < BLOCK
    low2 = lax.broadcasted_iota(jnp.int32, (BLOCK, 128), 1) < BLOCK
    r = lax.broadcasted_iota(jnp.int32, (BLOCK, BLOCK), 0)
    c = lax.broadcasted_iota(jnp.int32, (BLOCK, BLOCK), 1)
    place = (c == (r % 2) * ROWS + r // 2).astype(jnp.float32).astype(jnp.bfloat16)
    r = lax.broadcasted_iota(jnp.int32, (BLOCK, 128), 0)
    c = lax.broadcasted_iota(jnp.int32, (BLOCK, 128), 1)
    v = (r // HALF) % 2
    lane = v * BLOCK + 2 * ((r // ROWS) * HALF + r % HALF) + v
    pick = (c == lane).astype(jnp.float32).astype(jnp.bfloat16)
    spread_rows(lambda t: ref[pl.ds(base, GROUP), t * 128 : (t + 1) * 128], rows, 0)
    for i in range(0, GROUP, 2):
        ordered = []
        for j in (i, i + 1):
            own = piece(rows, j)
            turned = pltpu.roll(own, BLOCK, 1)
            ordered.append(
                jnp.concatenate(
                    [jnp.where(low, own, turned), jnp.where(low, turned, own)], axis=0
                ).astype(jnp.bfloat16)
            )
            if lefts is not None:
                stacked = jnp.concatenate([own, turned], axis=0)
                left = lax.dot_general(
                    pick, stacked.astype(jnp.bfloat16), (((1,), (1,)), ((), ())),
                    preferred_element_type=jnp.float32,
                )
                lefts[base + j] = left.astype(jnp.bfloat16)
        placed = jnp.dot(
            place, jnp.concatenate(ordered, axis=1), preferred_element_type=jnp.float32
        )
        for j in (0, 1):
            twice = placed[:, j * 128 : (j + 1) * 128]
            at_low = jnp.where(low2, twice, 0.0).astype(jnp.bfloat16)
            at_high = jnp.where(low2, 0.0, twice).astype(jnp.bfloat16)
            weights[slot0 + i + j, :BLOCK, :128] = at_low
            weights[slot0 + i + j, :BLOCK, 128:] = at_high
            weights[slot0 + i + j, BLOCK:, :128] = at_high
            weights[slot0 + i + j, BLOCK:, 128:] = at_low


def product_kernel(a_ref, p_ref, q_out, left_ref, face_ref, couples, q, rows, weights, sems):
    step = pl.program_id(0)
    start = pl.multiple_of(step * GROUP, GROUP)
    spread_weights(p_ref, start, rows, weights, start, left_ref)
    for k in range(PAIRS):
        spread_rows(
            lambda t: a_ref[k, :, t * 128 : (t + 1) * 128], rows, k * (GROUP * PITCH)
        )

    def lay(i, _):
        for k in range(PAIRS):
            couples[k, step * GROUP + i] = piece(rows, k * GROUP + i).astype(jnp.bfloat16)
        return 0

    lax.fori_loop(0, GROUP, lay, 0, unroll=4)

    @pl.when(step == pl.num_programs(0) - 1)
    def _multiply():
        plane = EX * EY

        def copy(n):
            span = pl.ds(n * GROUP, GROUP)
            return pltpu.make_async_copy(q.at[span], q_out.at[span], sems.at[n])

        behind = plane // GROUP

        for z in range(EZ):
            for g in range(plane // GROUP):
                base = z * plane + g * GROUP
                def neighbour(i, _):
                    j = base + i
                    x = j % EX
                    y = (j // EX) % EY
                    inside = (
                        None, x < EX - 1, x > 0, y < EY - 1, y > 0,
                        z < EZ - 1 or None, z > 0 or None,
                    )
                    away = (0, 1, -1, EX, -EX, plane, -plane)
                    here = [k for k in range(PAIRS) if k < 5 or inside[k]]
                    owners = [
                        j + away[k] if inside[k] is None or k >= 5
                        else jnp.where(inside[k], j + away[k], E_DEV)
                        for k in here
                    ]
                    left = jnp.concatenate(
                        [couples[k, e] for k, e in zip(here, owners)], axis=0
                    )
                    found = jnp.dot(left, weights[j], preferred_element_type=jnp.float32)
                    found = found.astype(jnp.bfloat16)
                    for n, (k, e) in enumerate(zip(here, owners)):
                        own = found[n * ROWS : (n + 1) * ROWS]
                        q[e, :ROWS, k * 128 : (k + 1) * 128] = own[:, :128]
                        q[e, ROWS:, k * 128 : (k + 1) * 128] = own[:, 128:]
                    return 0

                lax.fori_loop(0, GROUP, neighbour, 0, unroll=4)
                if base // GROUP >= behind:
                    copy(base // GROUP - behind).start()
        for n in range(E_DEV // GROUP - behind, E_DEV // GROUP):
            copy(n).start()
        for n in range(FACE):
            outer, x = divmod(n, EX)
            face_ref[n] = couples[3, outer * plane + x]
            face_ref[FACE + n] = couples[4, outer * plane + plane - EX + x]
            face_ref[2 * FACE + n] = couples[5, n]
            face_ref[3 * FACE + n] = couples[6, E_DEV - plane + n]
        for n in range(E_DEV // GROUP):
            copy(n).wait()


def add_terms(step, half, target_ref, lefts, q_ref, acc):
    low = lax.broadcasted_iota(jnp.int32, (HALF, PAIRS * 128), 1) % 128 < BLOCK

    def element(i, _):
        e = step * GROUP + i
        x = e % EX
        y = (e // EX) % EY
        z = e // (EX * EY)
        inside = (None, x > 0, x < EX - 1, y > 0, y < EY - 1, z > 0, z < EZ - 1)
        both = jnp.dot(
            lefts[e, half * ROWS : (half + 1) * ROWS, :], q_ref[i],
            preferred_element_type=jnp.float32,
        )
        terms = jnp.where(low, both[:HALF], both[HALF:])
        terms = terms.astype(jnp.bfloat16).astype(jnp.float32)
        for k in range(PAIRS):
            target = target_ref[e * PAIRS + k]
            if inside[k] is not None:
                target = jnp.where(inside[k], target, OWNERS * CB_DEV)
            acc[target] += terms[:, k * 128 : (k + 1) * 128]
        return 0

    lax.fori_loop(0, GROUP, element, 0, unroll=4)


def add_face_terms(step, half, target_ref, lefts, qh_ref, acc):
    low = lax.broadcasted_iota(jnp.int32, (HALF, 128), 1) < BLOCK
    plane = EX * EY
    face = step // (FACE // GROUP)

    def pair(i, _):
        n = step % (FACE // GROUP) * GROUP + i
        column = n // EX * plane + n % EX
        e = jnp.where(
            face < 2, column + face * (plane - EX), n + (face - 2) * (E_DEV - plane)
        )
        both = jnp.dot(
            lefts[e, half * ROWS : (half + 1) * ROWS, :], qh_ref[step * GROUP + i],
            preferred_element_type=jnp.float32,
        )
        term = jnp.where(low, both[:HALF], both[HALF:])
        acc[target_ref[e * PAIRS + 3 + face]] += term.astype(jnp.bfloat16).astype(jnp.float32)
        return 0

    lax.fori_loop(0, GROUP, pair, 0, unroll=8)


def drain(acc, stage, sems, outs):
    places = []
    for out in outs:
        places += [out.at[i] for i in range(out.shape[0])]
    copies = []
    for n in range(SLOTS):
        buffer = n % BUFFERS
        if n >= BUFFERS:
            copies[n - BUFFERS].wait()

        def cast(i, _):
            blocks = acc[pl.ds(n * SLOT + i * 16, 16)]
            stage[buffer, pl.ds(i * 16, 16)] = blocks.astype(jnp.bfloat16)
            return 0

        lax.fori_loop(0, SLOT // 16, cast, 0)
        copy = pltpu.make_async_copy(stage.at[buffer], places[n], sems.at[buffer])
        copy.start()
        copies.append(copy)
    for copy in copies[-BUFFERS:]:
        copy.wait()


def first_kernel(target_ref, left_ref, q_ref, face_ref, ym_ref, yp_ref, zm_ref, zp_ref, *refs):
    qh_ref, *outs = refs[:11]
    acc, stage, sems, weights, rows = refs[11:]
    step = pl.program_id(0)

    @pl.when(step == 0)
    def _clear():
        clear(acc)

    groups = FACE // GROUP
    for f, ref in enumerate((ym_ref, yp_ref, zm_ref, zp_ref)):

        @pl.when(step // groups == f)
        def _weights():
            base = pl.multiple_of(step % groups * GROUP, GROUP)
            spread_weights(ref, base, rows, weights, 0, None)

    def multiply(i, _):
        n = step * GROUP + i
        found = jnp.dot(face_ref[n], weights[i], preferred_element_type=jnp.float32)
        found = found.astype(jnp.bfloat16)
        qh_ref[n, :ROWS, :] = found[:, :128]
        qh_ref[n, ROWS:, :] = found[:, 128:]
        return 0

    lax.fori_loop(0, GROUP, multiply, 0, unroll=8)
    add_face_terms(step, 0, target_ref, left_ref, qh_ref, acc)
    add_terms(step, 0, target_ref, left_ref, q_ref, acc)

    @pl.when(step == pl.num_programs(0) - 1)
    def _drain():
        drain(acc, stage, sems, outs)


def second_kernel(target_ref, left_ref, q_ref, qh_ref, *refs):
    outs = refs[:10]
    acc, stage, sems = refs[10:]
    step = pl.program_id(0)

    @pl.when(step == 0)
    def _clear():
        clear(acc)

    add_face_terms(step, 1, target_ref, left_ref, qh_ref, acc)
    add_terms(step, 1, target_ref, left_ref, q_ref, acc)

    @pl.when(step == pl.num_programs(0) - 1)
    def _drain():
        drain(acc, stage, sems, outs)


VMEM = pl.BlockSpec(memory_space=pltpu.VMEM)
SMEM = pl.BlockSpec(memory_space=pltpu.SMEM)
HBM = pl.BlockSpec(memory_space=pl.ANY)
Q_SPEC = pl.BlockSpec((GROUP, BLOCK, PAIRS * 128), lambda i: (i, 0, 0))
PACKS = [
    jax.ShapeDtypeStruct((n, SLOT, HALF, 128), jnp.bfloat16) for n in (2, 2, 1, 1, 2) * 2
]
SUMS = [
    pltpu.VMEM((OWNERS * CB_DEV + 1, HALF, 128), jnp.float32),
    pltpu.VMEM((BUFFERS, SLOT, HALF, 128), jnp.bfloat16),
    pltpu.SemaphoreType.DMA((BUFFERS,)),
]
WEIGHTS = pltpu.VMEM((GROUP, 128, 256), jnp.bfloat16)


def params():
    return pltpu.CompilerParams(
        dimension_semantics=("arbitrary",), vmem_limit_bytes=48 * 1024 * 1024
    )


def cost(megabytes):
    return pl.CostEstimate(flops=10**10, bytes_accessed=megabytes * 10**6, transcendentals=0)


def local_products(a, p):
    return pl.pallas_call(
        product_kernel,
        grid=(E_DEV // GROUP,),
        in_specs=[pl.BlockSpec((PAIRS, GROUP, SQUARE), lambda i: (0, i, 0)), VMEM],
        out_specs=[HBM, VMEM, VMEM],
        out_shape=[
            jax.ShapeDtypeStruct((E_DEV, BLOCK, PAIRS * 128), jnp.bfloat16),
            jax.ShapeDtypeStruct((E_DEV, BLOCK, BLOCK), jnp.bfloat16),
            jax.ShapeDtypeStruct((4 * FACE, ROWS, 128), jnp.bfloat16),
        ],
        scratch_shapes=[
            pltpu.VMEM((PAIRS, E_DEV + 1, ROWS, 128), jnp.bfloat16),
            pltpu.VMEM((E_DEV + 1, BLOCK, PAIRS * 128), jnp.bfloat16),
            pltpu.VMEM((PAIRS * GROUP * PITCH + 8, 128), jnp.float32),
            pltpu.VMEM((E_DEV, 128, 256), jnp.bfloat16),
            pltpu.SemaphoreType.DMA((E_DEV // GROUP,)),
        ],
        compiler_params=params(),
        cost_estimate=cost(60),
        name="local_products",
    )(a, p)


def first_half(target, lefts, q, face, halos):
    found = pl.pallas_call(
        first_kernel,
        grid=(E_DEV // GROUP,),
        in_specs=[SMEM, VMEM, Q_SPEC, VMEM, VMEM, VMEM, VMEM, VMEM],
        out_specs=[VMEM] + [HBM] * len(PACKS),
        out_shape=[jax.ShapeDtypeStruct((4 * FACE, BLOCK, 128), jnp.bfloat16)] + PACKS,
        scratch_shapes=SUMS + [WEIGHTS, pltpu.VMEM((GROUP * PITCH + 8, 128), jnp.float32)],
        compiler_params=params(),
        cost_estimate=cost(60),
        name="first_half",
    )(target, lefts, q, face, *halos)
    return found[0], found[1:]


def second_half(target, lefts, q, qh):
    return pl.pallas_call(
        second_kernel,
        grid=(E_DEV // GROUP,),
        in_specs=[SMEM, VMEM, Q_SPEC, VMEM],
        out_specs=[HBM] * len(PACKS),
        out_shape=PACKS,
        scratch_shapes=SUMS,
        compiler_params=params(),
        cost_estimate=cost(60),
        name="second_half",
    )(target, lefts, q, qh)


def faces(p):
    brick = p.reshape(EZ, EY, EX, SQUARE)
    found = []
    for axis, dim in (("dom", 1), ("slab", 0)):
        size = lax.axis_size(axis)
        up = [(i, i + 1) for i in range(size - 1)]
        down = [(j, i) for i, j in up]
        length = brick.shape[dim]
        last = lax.slice_in_dim(brick, length - 1, length, axis=dim).reshape(FACE, SQUARE)
        first = lax.slice_in_dim(brick, 0, 1, axis=dim).reshape(FACE, SQUARE)
        found += [lax.ppermute(last, axis, up), lax.ppermute(first, axis, down)]
    return found


def sum_places(dest_rank, dest_block):
    me = lax.axis_index("dom")
    rank = dest_rank.reshape(-1)
    block = dest_block.reshape(-1)
    dx = (rank - me) % SIDE
    dy = (rank // SIDE - me // SIDE) % SIDE
    which = block // (2 * PART)
    part = (block // PART) % 2
    hops = jnp.where(which == 0, dx, dy)
    other = jnp.where(which == 0, dy, dx)
    slot = (SLOT_OF >> (4 * (2 * hops + part))) & 7
    return ((which * (SLOTS // 2) + slot) * SIDE + other) * PART + block % PART


def ring_perms():
    def moved(dx, dy):
        return [
            (y * SIDE + x, (y + dy) % SIDE * SIDE + (x + dx) % SIDE)
            for y in range(SIDE)
            for x in range(SIDE)
        ]

    return (moved(1, 0), moved(-1, 0)), (moved(0, 1), moved(0, -1))


def added(*parts):
    total = parts[0].astype(jnp.float32)
    for part in parts[1:]:
        total = total + part.astype(jnp.float32)
    return total


def join(keep, arrived):
    return added(keep, arrived).astype(jnp.bfloat16)


def exchange(halves):
    along_x, along_y = ring_perms()
    sets = ((0, along_x, along_y), (5, along_y, along_x))

    def send(pair, perms):
        return [lax.ppermute(v, "dom", perm) for v, perm in zip(pair, perms)]

    first = [
        lax.optimization_barrier([send(packs[at : at + 2], one) for at, one, _ in sets])
        for packs in halves
    ]
    second = []
    for packs, arrived in zip(halves, first):
        row = []
        for (at, one, _), (r1, l1) in zip(sets, arrived):
            row.append(send((join(packs[at + 2][0], r1[0]), join(packs[at + 3][0], l1[0])), one))
        second.append(lax.optimization_barrier(row))
    shape = (SIDE, PART, HALF, 128)
    sums = [[], []]
    for packs, one, two in zip(halves, first, second):
        for n, ((at, _, _), (r1, l1), (r2, l2)) in enumerate(zip(sets, one, two)):
            own = packs[at + 4]
            sums[n].append(
                (added(own[0], r2, l1[1]).reshape(shape), added(own[1], r1[1], l2).reshape(shape))
            )
    third, kept = [], []
    for (_, _, two), parts in zip(sets, sums):
        r, l = ([jnp.stack([h[p][n] for h in parts]) for n in range(SIDE)] for p in range(2))
        r16, l16 = ([v.astype(jnp.bfloat16) for v in w] for w in (r, l))
        kept.append((r[0], l[0], r16[1], l16[3]))
        third.append(send((jnp.stack([r16[2], l16[1]]), jnp.stack([l16[2], r16[3]])), two))
    third = lax.optimization_barrier(third)
    found = []
    for (_, _, two), (right, left, keep_right, keep_left), (r1, l1) in zip(sets, kept, third):
        fourth = send((join(keep_right, r1[0]), join(keep_left, l1[0])), two)
        found += [right, left, r1, l1, *fourth]
    return found


def finish_kernel(*refs):
    *ins, out_ref, scratch = refs
    for which in range(2):
        own_right, own_left, r1, l1, r2, l2 = ins[6 * which : 6 * which + 6]
        for half in range(2):
            parts = (
                (own_right[half], r2[half], l1[1, half]),
                (own_left[half], r1[1, half], l2[half]),
            )
            for part, pieces in enumerate(parts):
                total = added(*pieces)
                for c in range(PART):
                    scratch[c * FLAT_PITCH : c * FLAT_PITCH + HALF, :] = total[c]
                rows = pl.ds((2 * which + part) * PART, PART)
                for u in range(HALF):
                    t = half * HALF + u
                    out_ref[rows, t * 128 : (t + 1) * 128] = scratch[
                        pl.ds(u, PART, stride=FLAT_PITCH), :
                    ]


def finish(parts):
    return pl.pallas_call(
        finish_kernel,
        in_specs=[VMEM] * len(parts),
        out_specs=VMEM,
        out_shape=jax.ShapeDtypeStruct((CB_DEV, SQUARE), jnp.float32),
        scratch_shapes=[pltpu.VMEM((PART * FLAT_PITCH + 8, 128), jnp.float32)],
        name="finish",
    )(*parts)


def on_device(a_blocks, p_blocks, dest_rank, dest_block):
    halos = faces(p_blocks)
    target = sum_places(dest_rank, dest_block)
    q, lefts, face = local_products(jnp.swapaxes(a_blocks, 0, 1), p_blocks)
    qh, first = first_half(target, lefts, q, face, halos)
    second = second_half(target, lefts, q, qh)
    return finish(exchange((first, second)))


def solution(mesh):
    return jax.shard_map(
        on_device,
        mesh=mesh,
        in_specs=(
            P(("slab", "dom"), None, None),
            P(("slab", "dom"), None),
            P(("slab", "dom"), None),
            P(("slab", "dom"), None),
        ),
        out_specs=P(("slab", "dom"), None),
        check_vma=False,
    )
```

```python
import jax
import jax.numpy as jnp
from jax import lax
from jax.experimental import pallas as pl
from jax.experimental.pallas import tpu as pltpu
from jax.sharding import PartitionSpec as P

BLOCK = 64
PAIRS = 7
EX = 8
EY = 4
EZ = 4
E_DEV = EX * EY * EZ
CB_DEV = 128
SQUARE = BLOCK * BLOCK
ROWS = SQUARE // 128
HALF = ROWS // 2
PITCH = 33
FLAT_PITCH = 17
GROUP = 16
FACE = 32
SIDE = 4
OWNERS = SIDE * SIDE
PART = CB_DEV // 4
SLOT = SIDE * PART
SLOTS = OWNERS * CB_DEV // SLOT
BUFFERS = 4
SLOT_OF = 0x53201476


def spread_rows(flat, scratch, base):
    for t in range(ROWS):
        scratch[pl.ds(base + t, GROUP, stride=PITCH), :] = flat(t).astype(jnp.float32)


def piece(scratch, index):
    return scratch[pl.ds(index * PITCH, ROWS), :]


def clear(acc):
    def body(i, _):
        acc[pl.ds(i * 16, 16)] = jnp.zeros((16, HALF, 128), jnp.float32)
        return 0

    lax.fori_loop(0, OWNERS * CB_DEV // 16, body, 0)


def spread_weights(ref, base, rows, weights, slot0, lefts):
    low = lax.broadcasted_iota(jnp.int32, (ROWS, 128), 1) < BLOCK
    low2 = lax.broadcasted_iota(jnp.int32, (BLOCK, 128), 1) < BLOCK
    r = lax.broadcasted_iota(jnp.int32, (BLOCK, BLOCK), 0)
    c = lax.broadcasted_iota(jnp.int32, (BLOCK, BLOCK), 1)
    place = (c == (r % 2) * ROWS + r // 2).astype(jnp.float32).astype(jnp.bfloat16)
    r = lax.broadcasted_iota(jnp.int32, (BLOCK, 128), 0)
    c = lax.broadcasted_iota(jnp.int32, (BLOCK, 128), 1)
    v = (r // HALF) % 2
    lane = v * BLOCK + 2 * ((r // ROWS) * HALF + r % HALF) + v
    pick = (c == lane).astype(jnp.float32).astype(jnp.bfloat16)
    spread_rows(lambda t: ref[pl.ds(base, GROUP), t * 128 : (t + 1) * 128], rows, 0)
    for i in range(0, GROUP, 2):
        ordered = []
        for j in (i, i + 1):
            own = piece(rows, j)
            turned = pltpu.roll(own, BLOCK, 1)
            ordered.append(
                jnp.concatenate(
                    [jnp.where(low, own, turned), jnp.where(low, turned, own)], axis=0
                ).astype(jnp.bfloat16)
            )
            if lefts is not None:
                stacked = jnp.concatenate([own, turned], axis=0)
                left = lax.dot_general(
                    pick, stacked.astype(jnp.bfloat16), (((1,), (1,)), ((), ())),
                    preferred_element_type=jnp.float32,
                )
                lefts[base + j] = left.astype(jnp.bfloat16)
        placed = jnp.dot(
            place, jnp.concatenate(ordered, axis=1), preferred_element_type=jnp.float32
        )
        for j in (0, 1):
            twice = placed[:, j * 128 : (j + 1) * 128]
            at_low = jnp.where(low2, twice, 0.0).astype(jnp.bfloat16)
            at_high = jnp.where(low2, 0.0, twice).astype(jnp.bfloat16)
            weights[slot0 + i + j, :BLOCK, :128] = at_low
            weights[slot0 + i + j, :BLOCK, 128:] = at_high
            weights[slot0 + i + j, BLOCK:, :128] = at_high
            weights[slot0 + i + j, BLOCK:, 128:] = at_low


def first_kernel(target_ref, a_ref, p_ref, ym_ref, yp_ref, zm_ref, zp_ref, *refs):
    q_out, left_out, qh_out, *outs = refs[:13]
    acc, stage, drain_sems, couples, q, rows, weights, left_ref, qh_ref, sems = refs[13:]
    step = pl.program_id(0)

    @pl.when(step == 0)
    def _clear():
        clear(acc)

    start = pl.multiple_of(step * GROUP, GROUP)
    spread_weights(p_ref, start, rows, weights, start, left_ref)
    for k in range(PAIRS):
        spread_rows(
            lambda t: a_ref[k, :, t * 128 : (t + 1) * 128], rows, k * (GROUP * PITCH)
        )

    def lay(i, _):
        for k in range(PAIRS):
            couples[k, step * GROUP + i] = piece(rows, k * GROUP + i).astype(jnp.bfloat16)
        return 0

    lax.fori_loop(0, GROUP, lay, 0, unroll=4)

    @pl.when(step == pl.num_programs(0) - 1)
    def _multiply():
        plane = EX * EY

        def copy(n):
            span = pl.ds(n * GROUP, GROUP)
            return pltpu.make_async_copy(q.at[span], q_out.at[span], sems.at[n])

        lefts_away = pltpu.make_async_copy(left_ref, left_out, sems.at[E_DEV // GROUP])
        faces_away = pltpu.make_async_copy(qh_ref, qh_out, sems.at[E_DEV // GROUP + 1])
        lefts_away.start()
        behind = plane // GROUP

        for z in range(EZ):
            for g in range(plane // GROUP):
                base = z * plane + g * GROUP
                def neighbour(i, _):
                    j = base + i
                    x = j % EX
                    y = (j // EX) % EY
                    inside = (
                        None, x < EX - 1, x > 0, y < EY - 1, y > 0,
                        z < EZ - 1 or None, z > 0 or None,
                    )
                    away = (0, 1, -1, EX, -EX, plane, -plane)
                    here = [k for k in range(PAIRS) if k < 5 or inside[k]]
                    owners = [
                        j + away[k] if inside[k] is None or k >= 5
                        else jnp.where(inside[k], j + away[k], E_DEV)
                        for k in here
                    ]
                    left = jnp.concatenate(
                        [couples[k, e] for k, e in zip(here, owners)], axis=0
                    )
                    found = jnp.dot(left, weights[j], preferred_element_type=jnp.float32)
                    found = found.astype(jnp.bfloat16)
                    for n, (k, e) in enumerate(zip(here, owners)):
                        own = found[n * ROWS : (n + 1) * ROWS]
                        q[e, :ROWS, k * 128 : (k + 1) * 128] = own[:, :128]
                        q[e, ROWS:, k * 128 : (k + 1) * 128] = own[:, 128:]
                    return 0

                lax.fori_loop(0, GROUP, neighbour, 0, unroll=8)
                if base // GROUP >= behind:
                    copy(base // GROUP - behind).start()
        for n in range(E_DEV // GROUP - behind, E_DEV // GROUP):
            copy(n).start()

        for f, ref in enumerate((ym_ref, yp_ref, zm_ref, zp_ref)):
            for g in range(FACE // GROUP):
                spread_weights(ref, g * GROUP, rows, weights, f * FACE + g * GROUP, None)

        def face_pair(n, _):
            column = n // EX * plane + n % EX
            elements = (column, column + plane - EX, n, n + E_DEV - plane)
            for f, e in enumerate(elements):
                found = jnp.dot(
                    couples[3 + f, e], weights[f * FACE + n], preferred_element_type=jnp.float32
                ).astype(jnp.bfloat16)
                qh_ref[f * FACE + n, :ROWS, :] = found[:, :128]
                qh_ref[f * FACE + n, ROWS:, :] = found[:, 128:]
            return 0

        lax.fori_loop(0, FACE, face_pair, 0, unroll=8)
        faces_away.start()

        def terms(n, _):
            add_face_terms(n, 0, target_ref, left_ref, qh_ref, acc)
            add_terms(n, 0, target_ref, left_ref, q.at[pl.ds(n * GROUP, GROUP)], acc)
            return 0

        lax.fori_loop(0, E_DEV // GROUP, terms, 0)
        drain(acc, stage, drain_sems, outs)
        for n in range(E_DEV // GROUP):
            copy(n).wait()
        lefts_away.wait()
        faces_away.wait()


def add_terms(step, half, target_ref, lefts, q_ref, acc):
    low = lax.broadcasted_iota(jnp.int32, (HALF, PAIRS * 128), 1) % 128 < BLOCK

    def element(i, _):
        e = step * GROUP + i
        x = e % EX
        y = (e // EX) % EY
        z = e // (EX * EY)
        inside = (None, x > 0, x < EX - 1, y > 0, y < EY - 1, z > 0, z < EZ - 1)
        both = jnp.dot(
            lefts[e, half * ROWS : (half + 1) * ROWS, :], q_ref[i],
            preferred_element_type=jnp.float32,
        )
        terms = jnp.where(low, both[:HALF], both[HALF:])
        terms = terms.astype(jnp.bfloat16).astype(jnp.float32)
        for k in range(PAIRS):
            target = target_ref[e * PAIRS + k]
            if inside[k] is not None:
                target = jnp.where(inside[k], target, OWNERS * CB_DEV)
            acc[target] += terms[:, k * 128 : (k + 1) * 128]
        return 0

    lax.fori_loop(0, GROUP, element, 0, unroll=8)


def add_face_terms(step, half, target_ref, lefts, qh_ref, acc):
    low = lax.broadcasted_iota(jnp.int32, (HALF, 128), 1) < BLOCK
    plane = EX * EY
    face = step // (FACE // GROUP)

    def pair(i, _):
        n = step % (FACE // GROUP) * GROUP + i
        column = n // EX * plane + n % EX
        e = jnp.where(
            face < 2, column + face * (plane - EX), n + (face - 2) * (E_DEV - plane)
        )
        both = jnp.dot(
            lefts[e, half * ROWS : (half + 1) * ROWS, :], qh_ref[step * GROUP + i],
            preferred_element_type=jnp.float32,
        )
        term = jnp.where(low, both[:HALF], both[HALF:])
        acc[target_ref[e * PAIRS + 3 + face]] += term.astype(jnp.bfloat16).astype(jnp.float32)
        return 0

    lax.fori_loop(0, GROUP, pair, 0, unroll=16)


def drain(acc, stage, sems, outs):
    places = []
    for out in outs:
        places += [out.at[i] for i in range(out.shape[0])]
    copies = []
    for n in range(SLOTS):
        buffer = n % BUFFERS
        if n >= BUFFERS:
            copies[n - BUFFERS].wait()

        def cast(i, _):
            blocks = acc[pl.ds(n * SLOT + i * 16, 16)]
            stage[buffer, pl.ds(i * 16, 16)] = blocks.astype(jnp.bfloat16)
            return 0

        lax.fori_loop(0, SLOT // 16, cast, 0)
        copy = pltpu.make_async_copy(stage.at[buffer], places[n], sems.at[buffer])
        copy.start()
        copies.append(copy)
    for copy in copies[-BUFFERS:]:
        copy.wait()


def second_kernel(target_ref, left_ref, q_ref, qh_ref, *refs):
    outs = refs[:10]
    acc, stage, sems = refs[10:]
    step = pl.program_id(0)

    @pl.when(step == 0)
    def _clear():
        clear(acc)

    add_face_terms(step, 1, target_ref, left_ref, qh_ref, acc)
    add_terms(step, 1, target_ref, left_ref, q_ref, acc)

    @pl.when(step == pl.num_programs(0) - 1)
    def _drain():
        drain(acc, stage, sems, outs)


VMEM = pl.BlockSpec(memory_space=pltpu.VMEM)
SMEM = pl.BlockSpec(memory_space=pltpu.SMEM)
HBM = pl.BlockSpec(memory_space=pl.ANY)
Q_SPEC = pl.BlockSpec((GROUP, BLOCK, PAIRS * 128), lambda i: (i, 0, 0))
PACKS = [
    jax.ShapeDtypeStruct((n, SLOT, HALF, 128), jnp.bfloat16) for n in (2, 2, 1, 1, 2) * 2
]
SUMS = [
    pltpu.VMEM((OWNERS * CB_DEV + 1, HALF, 128), jnp.float32),
    pltpu.VMEM((BUFFERS, SLOT, HALF, 128), jnp.bfloat16),
    pltpu.SemaphoreType.DMA((BUFFERS,)),
]


def params(megabytes):
    return pltpu.CompilerParams(
        dimension_semantics=("arbitrary",), vmem_limit_bytes=megabytes * 1024 * 1024
    )


def cost(megabytes):
    return pl.CostEstimate(flops=10**10, bytes_accessed=megabytes * 10**6, transcendentals=0)


def first_half(target, a, p, halos):
    found = pl.pallas_call(
        first_kernel,
        grid=(E_DEV // GROUP,),
        in_specs=[
            SMEM,
            pl.BlockSpec((PAIRS, GROUP, SQUARE), lambda i: (0, i, 0)),
            VMEM, VMEM, VMEM, VMEM, VMEM,
        ],
        out_specs=[HBM] * (3 + len(PACKS)),
        out_shape=[
            jax.ShapeDtypeStruct((E_DEV, BLOCK, PAIRS * 128), jnp.bfloat16),
            jax.ShapeDtypeStruct((E_DEV, BLOCK, BLOCK), jnp.bfloat16),
            jax.ShapeDtypeStruct((4 * FACE, BLOCK, 128), jnp.bfloat16),
        ]
        + PACKS,
        scratch_shapes=SUMS
        + [
            pltpu.VMEM((PAIRS, E_DEV + 1, ROWS, 128), jnp.bfloat16),
            pltpu.VMEM((E_DEV + 1, BLOCK, PAIRS * 128), jnp.bfloat16),
            pltpu.VMEM((PAIRS * GROUP * PITCH + 8, 128), jnp.float32),
            pltpu.VMEM((E_DEV, 128, 256), jnp.bfloat16),
            pltpu.VMEM((E_DEV, BLOCK, BLOCK), jnp.bfloat16),
            pltpu.VMEM((4 * FACE, BLOCK, 128), jnp.bfloat16),
            pltpu.SemaphoreType.DMA((E_DEV // GROUP + 2,)),
        ],
        compiler_params=params(62),
        cost_estimate=cost(60),
        name="first_half",
    )(target, a, p, *halos)
    return found[0], found[1], found[2], found[3:]


def second_half(target, lefts, q, qh):
    return pl.pallas_call(
        second_kernel,
        grid=(E_DEV // GROUP,),
        in_specs=[SMEM, VMEM, Q_SPEC, VMEM],
        out_specs=[HBM] * len(PACKS),
        out_shape=PACKS,
        scratch_shapes=SUMS,
        compiler_params=params(48),
        cost_estimate=cost(60),
        name="second_half",
    )(target, lefts, q, qh)


def faces(p):
    brick = p.reshape(EZ, EY, EX, SQUARE)
    found = []
    for axis, dim in (("dom", 1), ("slab", 0)):
        size = lax.axis_size(axis)
        up = [(i, i + 1) for i in range(size - 1)]
        down = [(j, i) for i, j in up]
        length = brick.shape[dim]
        last = lax.slice_in_dim(brick, length - 1, length, axis=dim).reshape(FACE, SQUARE)
        first = lax.slice_in_dim(brick, 0, 1, axis=dim).reshape(FACE, SQUARE)
        found += [lax.ppermute(last, axis, up), lax.ppermute(first, axis, down)]
    return found


def sum_places(dest_rank, dest_block):
    me = lax.axis_index("dom")
    rank = dest_rank.reshape(-1)
    block = dest_block.reshape(-1)
    dx = (rank - me) % SIDE
    dy = (rank // SIDE - me // SIDE) % SIDE
    which = block // (2 * PART)
    part = (block // PART) % 2
    hops = jnp.where(which == 0, dx, dy)
    other = jnp.where(which == 0, dy, dx)
    slot = (SLOT_OF >> (4 * (2 * hops + part))) & 7
    return ((which * (SLOTS // 2) + slot) * SIDE + other) * PART + block % PART


def ring_perms():
    def moved(dx, dy):
        return [
            (y * SIDE + x, (y + dy) % SIDE * SIDE + (x + dx) % SIDE)
            for y in range(SIDE)
            for x in range(SIDE)
        ]

    return (moved(1, 0), moved(-1, 0)), (moved(0, 1), moved(0, -1))


def added(*parts):
    total = parts[0].astype(jnp.float32)
    for part in parts[1:]:
        total = total + part.astype(jnp.float32)
    return total


def join(keep, arrived):
    return added(keep, arrived).astype(jnp.bfloat16)


def exchange(halves):
    along_x, along_y = ring_perms()
    sets = ((0, along_x, along_y), (5, along_y, along_x))

    def send(pair, perms):
        return [lax.ppermute(v, "dom", perm) for v, perm in zip(pair, perms)]

    first = [
        lax.optimization_barrier([send(packs[at : at + 2], one) for at, one, _ in sets])
        for packs in halves
    ]
    second = []
    for packs, arrived in zip(halves, first):
        row = []
        for (at, one, _), (r1, l1) in zip(sets, arrived):
            row.append(send((join(packs[at + 2][0], r1[0]), join(packs[at + 3][0], l1[0])), one))
        second.append(lax.optimization_barrier(row))
    shape = (SIDE, PART, HALF, 128)
    sums = [[], []]
    for packs, one, two in zip(halves, first, second):
        for n, ((at, _, _), (r1, l1), (r2, l2)) in enumerate(zip(sets, one, two)):
            own = packs[at + 4]
            sums[n].append(
                (added(own[0], r2, l1[1]).reshape(shape), added(own[1], r1[1], l2).reshape(shape))
            )
    third, kept = [], []
    for (_, _, two), parts in zip(sets, sums):
        r, l = ([jnp.stack([h[p][n] for h in parts]) for n in range(SIDE)] for p in range(2))
        r16, l16 = ([v.astype(jnp.bfloat16) for v in w] for w in (r, l))
        kept.append((r[0], l[0], r16[1], l16[3]))
        third.append(send((jnp.stack([r16[2], l16[1]]), jnp.stack([l16[2], r16[3]])), two))
    third = lax.optimization_barrier(third)
    found = []
    for (_, _, two), (right, left, keep_right, keep_left), (r1, l1) in zip(sets, kept, third):
        fourth = send((join(keep_right, r1[0]), join(keep_left, l1[0])), two)
        found += [added(right, l1[1]), added(left, r1[1]), *fourth]
    return found


def finish_kernel(*refs):
    *ins, out_ref, scratch = refs
    for n in range(4):
        base = ins[4 * (n // 2) + n % 2]
        last = ins[4 * (n // 2) + 2 + n % 2]
        for half in range(2):
            total = added(base[half], last[half])
            for c in range(PART):
                scratch[c * FLAT_PITCH : c * FLAT_PITCH + HALF, :] = total[c]
            for u in range(HALF):
                t = half * HALF + u
                out_ref[n * PART : (n + 1) * PART, t * 128 : (t + 1) * 128] = scratch[
                    pl.ds(u, PART, stride=FLAT_PITCH), :
                ]


def finish(parts):
    return pl.pallas_call(
        finish_kernel,
        in_specs=[VMEM] * len(parts),
        out_specs=VMEM,
        out_shape=jax.ShapeDtypeStruct((CB_DEV, SQUARE), jnp.float32),
        scratch_shapes=[pltpu.VMEM((PART * FLAT_PITCH + 8, 128), jnp.float32)],
        name="finish",
    )(*parts)


def on_device(a_blocks, p_blocks, dest_rank, dest_block):
    halos = faces(p_blocks)
    target = sum_places(dest_rank, dest_block)
    q, lefts, qh, first = first_half(target, jnp.swapaxes(a_blocks, 0, 1), p_blocks, halos)
    second = second_half(target, lefts, q, qh)
    return finish(exchange((first, second)))


def solution(mesh):
    return jax.shard_map(
        on_device,
        mesh=mesh,
        in_specs=(
            P(("slab", "dom"), None, None),
            P(("slab", "dom"), None),
            P(("slab", "dom"), None),
            P(("slab", "dom"), None),
        ),
        out_specs=P(("slab", "dom"), None),
        check_vma=False,
    )
```

```python
import jax
import jax.numpy as jnp
from jax import lax
from jax.experimental import pallas as pl
from jax.experimental.pallas import tpu as pltpu
from jax.sharding import PartitionSpec as P

BLOCK = 64
PAIRS = 7
EX = 8
EY = 4
EZ = 4
E_DEV = EX * EY * EZ
CB_DEV = 128
SQUARE = BLOCK * BLOCK
ROWS = SQUARE // 128
HALF = ROWS // 2
PITCH = 33
FLAT_PITCH = 17
GROUP = 16
FACE = 32
SIDE = 4
OWNERS = SIDE * SIDE
PART = CB_DEV // 4
SLOT = SIDE * PART
SLOTS = OWNERS * CB_DEV // SLOT
BUFFERS = 4
SLOT_OF = 0x35204176


def spread_rows(flat, scratch, base):
    for t in range(ROWS):
        scratch[pl.ds(base + t, GROUP, stride=PITCH), :] = flat(t).astype(jnp.float32)


def piece(scratch, index):
    return scratch[pl.ds(index * PITCH, ROWS), :]


def clear(acc):
    def body(i, _):
        acc[pl.ds(i * 16, 16)] = jnp.zeros((16, HALF, 128), jnp.float32)
        return 0

    lax.fori_loop(0, OWNERS * CB_DEV // 16, body, 0)


def spread_weights(ref, base, rows, weights, slot0, lefts):
    low = lax.broadcasted_iota(jnp.int32, (ROWS, 128), 1) < BLOCK
    low2 = lax.broadcasted_iota(jnp.int32, (BLOCK, 128), 1) < BLOCK
    r = lax.broadcasted_iota(jnp.int32, (BLOCK, BLOCK), 0)
    c = lax.broadcasted_iota(jnp.int32, (BLOCK, BLOCK), 1)
    place = (c == (r % 2) * ROWS + r // 2).astype(jnp.float32).astype(jnp.bfloat16)
    r = lax.broadcasted_iota(jnp.int32, (BLOCK, 128), 0)
    c = lax.broadcasted_iota(jnp.int32, (BLOCK, 128), 1)
    v = (r // HALF) % 2
    lane = v * BLOCK + 2 * ((r // ROWS) * HALF + r % HALF) + v
    pick = (c == lane).astype(jnp.float32).astype(jnp.bfloat16)
    spread_rows(lambda t: ref[pl.ds(base, GROUP), t * 128 : (t + 1) * 128], rows, 0)
    for i in range(0, GROUP, 2):
        ordered = []
        for j in (i, i + 1):
            own = piece(rows, j)
            turned = pltpu.roll(own, BLOCK, 1)
            ordered.append(
                jnp.concatenate(
                    [jnp.where(low, own, turned), jnp.where(low, turned, own)], axis=0
                ).astype(jnp.bfloat16)
            )
            if lefts is not None:
                stacked = jnp.concatenate([own, turned], axis=0)
                left = lax.dot_general(
                    pick, stacked.astype(jnp.bfloat16), (((1,), (1,)), ((), ())),
                    preferred_element_type=jnp.float32,
                )
                lefts[base + j] = left.astype(jnp.bfloat16)
        placed = jnp.dot(
            place, jnp.concatenate(ordered, axis=1), preferred_element_type=jnp.float32
        )
        for j in (0, 1):
            twice = placed[:, j * 128 : (j + 1) * 128]
            at_low = jnp.where(low2, twice, 0.0).astype(jnp.bfloat16)
            at_high = jnp.where(low2, 0.0, twice).astype(jnp.bfloat16)
            weights[slot0 + i + j, :BLOCK, :128] = at_low
            weights[slot0 + i + j, :BLOCK, 128:] = at_high
            weights[slot0 + i + j, BLOCK:, :128] = at_high
            weights[slot0 + i + j, BLOCK:, 128:] = at_low


def first_kernel(target_ref, odd_ref, a_ref, p_ref, *refs):
    halos, (q_out, left_out, qh_out), outs = refs[:4], refs[4:7], refs[7:17]
    acc, stage, drain_sems, couples, q, rows, weights, left_ref, qh_ref, sems = refs[17:]
    step = pl.program_id(0)

    @pl.when(step == 0)
    def _clear():
        clear(acc)

    start = pl.multiple_of(step * GROUP, GROUP)
    spread_weights(p_ref, start, rows, weights, start, left_ref)
    for k in range(PAIRS):
        spread_rows(
            lambda t: a_ref[k, :, t * 128 : (t + 1) * 128], rows, k * (GROUP * PITCH)
        )

    def lay(i, _):
        for k in range(PAIRS):
            couples[k, step * GROUP + i] = piece(rows, k * GROUP + i).astype(jnp.bfloat16)
        return 0

    lax.fori_loop(0, GROUP, lay, 0, unroll=4)

    @pl.when(step == pl.num_programs(0) - 1)
    def _multiply():
        plane = EX * EY

        def copy(n):
            span = pl.ds(n * GROUP, GROUP)
            return pltpu.make_async_copy(q.at[span], q_out.at[span], sems.at[n])

        lefts_away = pltpu.make_async_copy(left_ref, left_out, sems.at[E_DEV // GROUP])
        faces_away = pltpu.make_async_copy(qh_ref, qh_out, sems.at[E_DEV // GROUP + 1])
        lefts_away.start()
        behind = plane // GROUP

        for z in range(EZ):
            for g in range(plane // GROUP):
                base = z * plane + g * GROUP
                def neighbour(i, _):
                    j = base + i
                    x = j % EX
                    y = (j // EX) % EY
                    inside = (
                        None, x < EX - 1, x > 0, y < EY - 1, y > 0,
                        z < EZ - 1 or None, z > 0 or None,
                    )
                    away = (0, 1, -1, EX, -EX, plane, -plane)
                    here = [k for k in range(PAIRS) if k < 5 or inside[k]]
                    owners = [
                        j + away[k] if inside[k] is None or k >= 5
                        else jnp.where(inside[k], j + away[k], E_DEV)
                        for k in here
                    ]
                    left = jnp.concatenate(
                        [couples[k, e] for k, e in zip(here, owners)], axis=0
                    )
                    found = jnp.dot(left, weights[j], preferred_element_type=jnp.float32)
                    found = found.astype(jnp.bfloat16)
                    for n, (k, e) in enumerate(zip(here, owners)):
                        own = found[n * ROWS : (n + 1) * ROWS]
                        q[e, :ROWS, k * 128 : (k + 1) * 128] = own[:, :128]
                        q[e, ROWS:, k * 128 : (k + 1) * 128] = own[:, 128:]
                    return 0

                lax.fori_loop(0, GROUP, neighbour, 0, unroll=8)
                if base // GROUP >= behind:
                    copy(base // GROUP - behind).start()
        for n in range(E_DEV // GROUP - behind, E_DEV // GROUP):
            copy(n).start()

        dom_odd, slab_odd = odd_ref[0], odd_ref[1]
        sides = (1 - dom_odd, dom_odd, 3 - slab_odd, 2 + slab_odd)
        for f, ref in zip(sides, halos):
            for g in range(FACE // GROUP):
                spread_weights(ref, g * GROUP, rows, weights, f * FACE + g * GROUP, None)

        def face_pair(n, _):
            column = n // EX * plane + n % EX
            elements = (column, column + plane - EX, n, n + E_DEV - plane)
            for f, e in enumerate(elements):
                found = jnp.dot(
                    couples[3 + f, e], weights[f * FACE + n], preferred_element_type=jnp.float32
                ).astype(jnp.bfloat16)
                qh_ref[f * FACE + n, :ROWS, :] = found[:, :128]
                qh_ref[f * FACE + n, ROWS:, :] = found[:, 128:]
            return 0

        lax.fori_loop(0, FACE, face_pair, 0, unroll=8)
        faces_away.start()

        def terms(n, _):
            add_face_terms(n, 0, target_ref, left_ref, qh_ref, acc)
            add_terms(n, 0, target_ref, left_ref, q.at[pl.ds(n * GROUP, GROUP)], acc)
            return 0

        lax.fori_loop(0, E_DEV // GROUP, terms, 0)
        drain(acc, stage, drain_sems, outs)
        for n in range(E_DEV // GROUP):
            copy(n).wait()
        lefts_away.wait()
        faces_away.wait()


def add_terms(step, half, target_ref, lefts, q_ref, acc):
    low = lax.broadcasted_iota(jnp.int32, (HALF, PAIRS * 128), 1) % 128 < BLOCK

    def element(i, _):
        e = step * GROUP + i
        x = e % EX
        y = (e // EX) % EY
        z = e // (EX * EY)
        inside = (None, x > 0, x < EX - 1, y > 0, y < EY - 1, z > 0, z < EZ - 1)
        both = jnp.dot(
            lefts[e, half * ROWS : (half + 1) * ROWS, :], q_ref[i],
            preferred_element_type=jnp.float32,
        )
        terms = jnp.where(low, both[:HALF], both[HALF:])
        terms = terms.astype(jnp.bfloat16).astype(jnp.float32)
        for k in range(PAIRS):
            target = target_ref[e * PAIRS + k]
            if inside[k] is not None:
                target = jnp.where(inside[k], target, OWNERS * CB_DEV)
            acc[target] += terms[:, k * 128 : (k + 1) * 128]
        return 0

    lax.fori_loop(0, GROUP, element, 0, unroll=8)


def add_face_terms(step, half, target_ref, lefts, qh_ref, acc):
    low = lax.broadcasted_iota(jnp.int32, (HALF, 128), 1) < BLOCK
    plane = EX * EY
    face = step // (FACE // GROUP)

    def pair(i, _):
        n = step % (FACE // GROUP) * GROUP + i
        column = n // EX * plane + n % EX
        e = jnp.where(
            face < 2, column + face * (plane - EX), n + (face - 2) * (E_DEV - plane)
        )
        both = jnp.dot(
            lefts[e, half * ROWS : (half + 1) * ROWS, :], qh_ref[step * GROUP + i],
            preferred_element_type=jnp.float32,
        )
        term = jnp.where(low, both[:HALF], both[HALF:])
        acc[target_ref[e * PAIRS + 3 + face]] += term.astype(jnp.bfloat16).astype(jnp.float32)
        return 0

    lax.fori_loop(0, GROUP, pair, 0, unroll=16)


def drain(acc, stage, sems, outs):
    places = []
    for out in outs:
        places += [out.at[i] for i in range(out.shape[0])]
    copies = []
    for n in range(SLOTS):
        buffer = n % BUFFERS
        if n >= BUFFERS:
            copies[n - BUFFERS].wait()

        def cast(i, _):
            blocks = acc[pl.ds(n * SLOT + i * 16, 16)]
            stage[buffer, pl.ds(i * 16, 16)] = blocks.astype(jnp.bfloat16)
            return 0

        lax.fori_loop(0, SLOT // 16, cast, 0)
        copy = pltpu.make_async_copy(stage.at[buffer], places[n], sems.at[buffer])
        copy.start()
        copies.append(copy)
    for copy in copies[-BUFFERS:]:
        copy.wait()


def second_kernel(target_ref, left_ref, q_ref, qh_ref, *refs):
    outs = refs[:10]
    acc, stage, sems = refs[10:]
    step = pl.program_id(0)

    @pl.when(step == 0)
    def _clear():
        clear(acc)

    add_face_terms(step, 1, target_ref, left_ref, qh_ref, acc)
    add_terms(step, 1, target_ref, left_ref, q_ref, acc)

    @pl.when(step == pl.num_programs(0) - 1)
    def _drain():
        drain(acc, stage, sems, outs)


VMEM = pl.BlockSpec(memory_space=pltpu.VMEM)
SMEM = pl.BlockSpec(memory_space=pltpu.SMEM)
HBM = pl.BlockSpec(memory_space=pl.ANY)
Q_SPEC = pl.BlockSpec((GROUP, BLOCK, PAIRS * 128), lambda i: (i, 0, 0))
PACKS = [
    jax.ShapeDtypeStruct((n, SLOT, HALF, 128), jnp.bfloat16) for n in (2, 2, 1, 1, 2) * 2
]
SUMS = [
    pltpu.VMEM((OWNERS * CB_DEV + 1, HALF, 128), jnp.float32),
    pltpu.VMEM((BUFFERS, SLOT, HALF, 128), jnp.bfloat16),
    pltpu.SemaphoreType.DMA((BUFFERS,)),
]


def params(megabytes):
    return pltpu.CompilerParams(
        dimension_semantics=("arbitrary",), vmem_limit_bytes=megabytes * 1024 * 1024
    )


def cost(megabytes):
    return pl.CostEstimate(flops=10**10, bytes_accessed=megabytes * 10**6, transcendentals=0)


def first_half(target, odd, a, p, halos):
    found = pl.pallas_call(
        first_kernel,
        grid=(E_DEV // GROUP,),
        in_specs=[
            SMEM,
            SMEM,
            pl.BlockSpec((PAIRS, GROUP, SQUARE), lambda i: (0, i, 0)),
            VMEM, VMEM, VMEM, VMEM, VMEM,
        ],
        out_specs=[HBM] * (3 + len(PACKS)),
        out_shape=[
            jax.ShapeDtypeStruct((E_DEV, BLOCK, PAIRS * 128), jnp.bfloat16),
            jax.ShapeDtypeStruct((E_DEV, BLOCK, BLOCK), jnp.bfloat16),
            jax.ShapeDtypeStruct((4 * FACE, BLOCK, 128), jnp.bfloat16),
        ]
        + PACKS,
        scratch_shapes=SUMS
        + [
            pltpu.VMEM((PAIRS, E_DEV + 1, ROWS, 128), jnp.bfloat16),
            pltpu.VMEM((E_DEV + 1, BLOCK, PAIRS * 128), jnp.bfloat16),
            pltpu.VMEM((PAIRS * GROUP * PITCH + 8, 128), jnp.float32),
            pltpu.VMEM((E_DEV, 128, 256), jnp.bfloat16),
            pltpu.VMEM((E_DEV, BLOCK, BLOCK), jnp.bfloat16),
            pltpu.VMEM((4 * FACE, BLOCK, 128), jnp.bfloat16),
            pltpu.SemaphoreType.DMA((E_DEV // GROUP + 2,)),
        ],
        compiler_params=params(62),
        cost_estimate=cost(60),
        name="first_half",
    )(target, odd, a, p, *halos)
    return found[0], found[1], found[2], found[3:]


def second_half(target, lefts, q, qh):
    return pl.pallas_call(
        second_kernel,
        grid=(E_DEV // GROUP,),
        in_specs=[SMEM, VMEM, Q_SPEC, VMEM],
        out_specs=[HBM] * len(PACKS),
        out_shape=PACKS,
        scratch_shapes=SUMS,
        compiler_params=params(48),
        cost_estimate=cost(60),
        name="second_half",
    )(target, lefts, q, qh)


def faces(p):
    brick = p.reshape(EZ, EY, EX, SQUARE)
    found = []
    for axis, dim in (("dom", 1), ("slab", 0)):
        size = lax.axis_size(axis)
        even = lax.axis_index(axis) % 2 == 0
        length = brick.shape[dim]
        last = lax.slice_in_dim(brick, length - 1, length, axis=dim).reshape(FACE, SQUARE)
        first = lax.slice_in_dim(brick, 0, 1, axis=dim).reshape(FACE, SQUARE)
        near = [(i, i ^ 1) for i in range(size)]
        far = [(i, (i + 1 ^ 1) - 1) for i in range(1, size - 1)]
        found.append(lax.ppermute(jnp.where(even, last, first), axis, near))
        found.append(lax.ppermute(jnp.where(even, first, last), axis, far))
    return found


def sum_places(dest_rank, dest_block):
    me = lax.axis_index("dom")
    away = dest_rank.reshape(-1) ^ me
    block = dest_block.reshape(-1)
    dx = away % SIDE
    dy = away // SIDE
    which = block // (2 * PART)
    part = (block // PART) % 2
    place = jnp.where(which == 0, dx, dy)
    other = jnp.where(which == 0, dy, dx)
    slot = (SLOT_OF >> (4 * (2 * place + part))) & 7
    return ((which * (SLOTS // 2) + slot) * SIDE + other) * PART + block % PART


def pair_perms():
    return [
        [[(i, i ^ (swap * stride)) for i in range(OWNERS)] for swap in (1, 3)]
        for stride in (1, SIDE)
    ]


def added(*parts):
    total = parts[0].astype(jnp.float32)
    for part in parts[1:]:
        total = total + part.astype(jnp.float32)
    return total


def join(keep, arrived):
    return added(keep, arrived).astype(jnp.bfloat16)


def exchange(halves):
    along_x, along_y = pair_perms()
    sets = ((0, along_x, along_y), (5, along_y, along_x))

    def send(pair, perms):
        return [lax.ppermute(v, "dom", perm) for v, perm in zip(pair, perms)]

    first = [
        lax.optimization_barrier([send(packs[at : at + 2], one) for at, one, _ in sets])
        for packs in halves
    ]
    second = []
    for packs, arrived in zip(halves, first):
        row = []
        for (at, one, _), (near, far) in zip(sets, arrived):
            joined = join(packs[at + 2][0], far[0]), join(packs[at + 3][0], near[0])
            row.append(send(joined, one))
        second.append(lax.optimization_barrier(row))
    shape = (SIDE, PART, HALF, 128)
    sums = [[], []]
    for packs, one, two in zip(halves, first, second):
        for n, ((at, _, _), (n1, f1), (n2, f2)) in enumerate(zip(sets, one, two)):
            own = packs[at + 4]
            sums[n].append(
                (added(own[0], n1[1], f2).reshape(shape), added(own[1], f1[1], n2).reshape(shape))
            )
    third, kept = [], []
    for (_, _, two), parts in zip(sets, sums):
        p0, p1 = ([jnp.stack([h[p][n] for h in parts]) for n in range(SIDE)] for p in range(2))
        q0, q1 = ([v.astype(jnp.bfloat16) for v in w] for w in (p0, p1))
        kept.append((p0[0], p1[0], q1[1], q0[3]))
        third.append(send((jnp.stack([q0[2], q0[1]]), jnp.stack([q1[2], q1[3]])), two))
    third = lax.optimization_barrier(third)
    joined = [
        (join(keep_near, far[0]), join(keep_far, near[0]))
        for (_, _, keep_near, keep_far), (near, far) in zip(kept, third)
    ]
    joined, third = lax.optimization_barrier((joined, third))
    found = []
    for (_, _, two), (own0, own1, _, _), (n1, f1), pair in zip(sets, kept, third, joined):
        n2, f2 = send(pair, two)
        found += [added(own0, n1[1]), added(own1, f1[1]), f2, n2]
    return found


def finish_kernel(*refs):
    *ins, out_ref, scratch = refs
    for n in range(4):
        base = ins[4 * (n // 2) + n % 2]
        last = ins[4 * (n // 2) + 2 + n % 2]
        for half in range(2):
            total = added(base[half], last[half])
            for c in range(PART):
                scratch[c * FLAT_PITCH : c * FLAT_PITCH + HALF, :] = total[c]
            for u in range(HALF):
                t = half * HALF + u
                out_ref[n * PART : (n + 1) * PART, t * 128 : (t + 1) * 128] = scratch[
                    pl.ds(u, PART, stride=FLAT_PITCH), :
                ]


def finish(parts):
    return pl.pallas_call(
        finish_kernel,
        in_specs=[VMEM] * len(parts),
        out_specs=VMEM,
        out_shape=jax.ShapeDtypeStruct((CB_DEV, SQUARE), jnp.float32),
        scratch_shapes=[pltpu.VMEM((PART * FLAT_PITCH + 8, 128), jnp.float32)],
        name="finish",
    )(*parts)


def on_device(a_blocks, p_blocks, dest_rank, dest_block):
    halos = faces(p_blocks)
    target = sum_places(dest_rank, dest_block)
    odd = jnp.stack([lax.axis_index(axis) % 2 for axis in ("dom", "slab")])
    a = jnp.swapaxes(a_blocks, 0, 1)
    q, lefts, qh, first = first_half(target, odd, a, p_blocks, halos)
    second = second_half(target, lefts, q, qh)
    return finish(exchange((first, second)))


def solution(mesh):
    return jax.shard_map(
        on_device,
        mesh=mesh,
        in_specs=(
            P(("slab", "dom"), None, None),
            P(("slab", "dom"), None),
            P(("slab", "dom"), None),
            P(("slab", "dom"), None),
        ),
        out_specs=P(("slab", "dom"), None),
        check_vma=False,
    )
```

```python
import jax
import jax.numpy as jnp
from jax import lax
from jax.experimental import pallas as pl
from jax.experimental.pallas import tpu as pltpu
from jax.sharding import PartitionSpec as P

BLOCK = 64
PAIRS = 7
EX = 8
EY = 4
EZ = 4
E_DEV = EX * EY * EZ
CB_DEV = 128
SQUARE = BLOCK * BLOCK
ROWS = SQUARE // 128
HALF = ROWS // 2
PITCH = 33
FLAT_PITCH = 17
GROUP = 16
FACE = 32
SIDE = 4
OWNERS = SIDE * SIDE
PART = CB_DEV // 4
SLOT = SIDE * PART
SLOTS = OWNERS * CB_DEV // SLOT
BUFFERS = 4
SLOT_OF = 0x35204176


def spread_rows(flat, scratch, base):
    for t in range(ROWS):
        scratch[pl.ds(base + t, GROUP, stride=PITCH), :] = flat(t).astype(jnp.float32)


def piece(scratch, index):
    return scratch[pl.ds(index * PITCH, ROWS), :]


def clear(acc):
    def body(i, _):
        acc[pl.ds(i * 16, 16)] = jnp.zeros((16, HALF, 128), jnp.float32)
        return 0

    lax.fori_loop(0, OWNERS * CB_DEV // 16, body, 0)


def spread_weights(ref, base, rows, weights, slot0, lefts):
    low = lax.broadcasted_iota(jnp.int32, (ROWS, 128), 1) < BLOCK
    low2 = lax.broadcasted_iota(jnp.int32, (BLOCK, 128), 1) < BLOCK
    r = lax.broadcasted_iota(jnp.int32, (BLOCK, BLOCK), 0)
    c = lax.broadcasted_iota(jnp.int32, (BLOCK, BLOCK), 1)
    place = (c == (r % 2) * ROWS + r // 2).astype(jnp.float32).astype(jnp.bfloat16)
    r = lax.broadcasted_iota(jnp.int32, (BLOCK, 128), 0)
    c = lax.broadcasted_iota(jnp.int32, (BLOCK, 128), 1)
    v = (r // HALF) % 2
    lane = v * BLOCK + 2 * ((r // ROWS) * HALF + r % HALF) + v
    pick = (c == lane).astype(jnp.float32).astype(jnp.bfloat16)
    spread_rows(lambda t: ref[pl.ds(base, GROUP), t * 128 : (t + 1) * 128], rows, 0)
    for i in range(0, GROUP, 2):
        ordered = []
        for j in (i, i + 1):
            own = piece(rows, j)
            turned = pltpu.roll(own, BLOCK, 1)
            ordered.append(
                jnp.concatenate(
                    [jnp.where(low, own, turned), jnp.where(low, turned, own)], axis=0
                ).astype(jnp.bfloat16)
            )
            if lefts is not None:
                stacked = jnp.concatenate([own, turned], axis=0)
                left = lax.dot_general(
                    pick, stacked.astype(jnp.bfloat16), (((1,), (1,)), ((), ())),
                    preferred_element_type=jnp.float32,
                )
                lefts[base + j] = left.astype(jnp.bfloat16)
        placed = jnp.dot(
            place, jnp.concatenate(ordered, axis=1), preferred_element_type=jnp.float32
        )
        for j in (0, 1):
            twice = placed[:, j * 128 : (j + 1) * 128]
            at_low = jnp.where(low2, twice, 0.0).astype(jnp.bfloat16)
            at_high = jnp.where(low2, 0.0, twice).astype(jnp.bfloat16)
            weights[slot0 + i + j, :BLOCK, :128] = at_low
            weights[slot0 + i + j, :BLOCK, 128:] = at_high
            weights[slot0 + i + j, BLOCK:, :128] = at_high
            weights[slot0 + i + j, BLOCK:, 128:] = at_low


def first_kernel(target_ref, odd_ref, a_ref, p_ref, *refs):
    halos, (q_out, left_out, qh_out), outs = refs[:4], refs[4:7], refs[7:17]
    acc, stage, drain_sems, couples, q, rows, weights, left_ref, qh_ref, near, sems = refs[17:]
    step = pl.program_id(0)

    fetches = [
        pltpu.make_async_copy(ref, near.at[f], sems.at[E_DEV // GROUP + 2 + f])
        for f, ref in enumerate(halos)
    ]

    @pl.when(step == 0)
    def _clear():
        for fetch in fetches:
            fetch.start()
        clear(acc)

    start = pl.multiple_of(step * GROUP, GROUP)
    spread_weights(p_ref, start, rows, weights, start, left_ref)
    for k in range(PAIRS):
        spread_rows(
            lambda t: a_ref[k, :, t * 128 : (t + 1) * 128], rows, k * (GROUP * PITCH)
        )

    def lay(i, _):
        for k in range(PAIRS):
            couples[k, step * GROUP + i] = piece(rows, k * GROUP + i).astype(jnp.bfloat16)
        return 0

    lax.fori_loop(0, GROUP, lay, 0, unroll=4)

    @pl.when(step == pl.num_programs(0) - 1)
    def _multiply():
        plane = EX * EY

        def copy(n):
            span = pl.ds(n * GROUP, GROUP)
            return pltpu.make_async_copy(q.at[span], q_out.at[span], sems.at[n])

        lefts_away = pltpu.make_async_copy(left_ref, left_out, sems.at[E_DEV // GROUP])
        faces_away = pltpu.make_async_copy(qh_ref, qh_out, sems.at[E_DEV // GROUP + 1])
        lefts_away.start()
        behind = plane // GROUP

        for z in range(EZ):
            for g in range(plane // GROUP):
                base = z * plane + g * GROUP
                def neighbour(i, _):
                    j = base + i
                    x = j % EX
                    y = (j // EX) % EY
                    inside = (
                        None, x < EX - 1, x > 0, y < EY - 1, y > 0,
                        z < EZ - 1 or None, z > 0 or None,
                    )
                    away = (0, 1, -1, EX, -EX, plane, -plane)
                    here = [k for k in range(PAIRS) if k < 5 or inside[k]]
                    owners = [
                        j + away[k] if inside[k] is None or k >= 5
                        else jnp.where(inside[k], j + away[k], E_DEV)
                        for k in here
                    ]
                    left = jnp.concatenate(
                        [couples[k, e] for k, e in zip(here, owners)], axis=0
                    )
                    found = jnp.dot(left, weights[j], preferred_element_type=jnp.float32)
                    found = found.astype(jnp.bfloat16)
                    for n, (k, e) in enumerate(zip(here, owners)):
                        own = found[n * ROWS : (n + 1) * ROWS]
                        q[e, :ROWS, k * 128 : (k + 1) * 128] = own[:, :128]
                        q[e, ROWS:, k * 128 : (k + 1) * 128] = own[:, 128:]
                    return 0

                lax.fori_loop(0, GROUP, neighbour, 0, unroll=GROUP)
                if base // GROUP >= behind:
                    copy(base // GROUP - behind).start()
        for n in range(E_DEV // GROUP - behind, E_DEV // GROUP):
            copy(n).start()

        dom_odd, slab_odd = odd_ref[0], odd_ref[1]
        sides = (1 - dom_odd, dom_odd, 3 - slab_odd, 2 + slab_odd)
        for n, f in enumerate(sides):
            fetches[n].wait()
            for g in range(FACE // GROUP):
                spread_weights(near.at[n], g * GROUP, rows, weights, f * FACE + g * GROUP, None)

        def face_pair(n, _):
            column = n // EX * plane + n % EX
            elements = (column, column + plane - EX, n, n + E_DEV - plane)
            for f, e in enumerate(elements):
                found = jnp.dot(
                    couples[3 + f, e], weights[f * FACE + n], preferred_element_type=jnp.float32
                ).astype(jnp.bfloat16)
                qh_ref[f * FACE + n, :ROWS, :] = found[:, :128]
                qh_ref[f * FACE + n, ROWS:, :] = found[:, 128:]
            return 0

        lax.fori_loop(0, FACE, face_pair, 0, unroll=8)
        faces_away.start()

        def terms(n, _):
            add_face_terms(n, 0, target_ref, left_ref, qh_ref, acc)
            add_terms(n, 0, target_ref, left_ref, q.at[pl.ds(n * GROUP, GROUP)], acc)
            return 0

        lax.fori_loop(0, E_DEV // GROUP, terms, 0)
        drain(acc, stage, drain_sems, outs)
        for n in range(E_DEV // GROUP):
            copy(n).wait()
        lefts_away.wait()
        faces_away.wait()


def add_terms(step, half, target_ref, lefts, q_ref, acc):
    low = lax.broadcasted_iota(jnp.int32, (HALF, PAIRS * 128), 1) % 128 < BLOCK

    def element(i, _):
        e = step * GROUP + i
        x = e % EX
        y = (e // EX) % EY
        z = e // (EX * EY)
        inside = (None, x > 0, x < EX - 1, y > 0, y < EY - 1, z > 0, z < EZ - 1)
        both = jnp.dot(
            lefts[e, half * ROWS : (half + 1) * ROWS, :], q_ref[i],
            preferred_element_type=jnp.float32,
        )
        terms = jnp.where(low, both[:HALF], both[HALF:])
        terms = terms.astype(jnp.bfloat16).astype(jnp.float32)
        for k in range(PAIRS):
            target = target_ref[e * PAIRS + k]
            if inside[k] is not None:
                target = jnp.where(inside[k], target, OWNERS * CB_DEV)
            acc[target] += terms[:, k * 128 : (k + 1) * 128]
        return 0

    lax.fori_loop(0, GROUP, element, 0, unroll=GROUP)


def add_face_terms(step, half, target_ref, lefts, qh_ref, acc):
    low = lax.broadcasted_iota(jnp.int32, (HALF, 128), 1) < BLOCK
    plane = EX * EY
    face = step // (FACE // GROUP)

    def pair(i, _):
        n = step % (FACE // GROUP) * GROUP + i
        column = n // EX * plane + n % EX
        e = jnp.where(
            face < 2, column + face * (plane - EX), n + (face - 2) * (E_DEV - plane)
        )
        both = jnp.dot(
            lefts[e, half * ROWS : (half + 1) * ROWS, :], qh_ref[step * GROUP + i],
            preferred_element_type=jnp.float32,
        )
        term = jnp.where(low, both[:HALF], both[HALF:])
        acc[target_ref[e * PAIRS + 3 + face]] += term.astype(jnp.bfloat16).astype(jnp.float32)
        return 0

    lax.fori_loop(0, GROUP, pair, 0, unroll=GROUP)


def drain(acc, stage, sems, outs):
    places = []
    for out in outs:
        places += [out.at[i] for i in range(out.shape[0])]
    copies = []
    for n in range(SLOTS):
        buffer = n % BUFFERS
        if n >= BUFFERS:
            copies[n - BUFFERS].wait()

        def cast(i, _):
            blocks = acc[pl.ds(n * SLOT + i * 16, 16)]
            stage[buffer, pl.ds(i * 16, 16)] = blocks.astype(jnp.bfloat16)
            return 0

        lax.fori_loop(0, SLOT // 16, cast, 0)
        copy = pltpu.make_async_copy(stage.at[buffer], places[n], sems.at[buffer])
        copy.start()
        copies.append(copy)
    for copy in copies[-BUFFERS:]:
        copy.wait()


def second_kernel(target_ref, left_in, q_ref, qh_in, *refs):
    outs = refs[:10]
    acc, stage, drain_sems, left_ref, qh_ref, sems = refs[10:]
    step = pl.program_id(0)

    @pl.when(step == 0)
    def _clear():
        lefts = pltpu.make_async_copy(left_in, left_ref, sems.at[0])
        faces = pltpu.make_async_copy(qh_in, qh_ref, sems.at[1])
        lefts.start()
        faces.start()
        clear(acc)
        lefts.wait()
        faces.wait()

    add_face_terms(step, 1, target_ref, left_ref, qh_ref, acc)
    add_terms(step, 1, target_ref, left_ref, q_ref, acc)

    @pl.when(step == pl.num_programs(0) - 1)
    def _drain():
        drain(acc, stage, drain_sems, outs)


VMEM = pl.BlockSpec(memory_space=pltpu.VMEM)
SMEM = pl.BlockSpec(memory_space=pltpu.SMEM)
HBM = pl.BlockSpec(memory_space=pl.ANY)
Q_SPEC = pl.BlockSpec((GROUP, BLOCK, PAIRS * 128), lambda i: (i, 0, 0))
PACKS = [
    jax.ShapeDtypeStruct((n, SLOT, HALF, 128), jnp.bfloat16) for n in (2, 2, 1, 1, 2) * 2
]
SUMS = [
    pltpu.VMEM((OWNERS * CB_DEV + 1, HALF, 128), jnp.float32),
    pltpu.VMEM((BUFFERS, SLOT, HALF, 128), jnp.bfloat16),
    pltpu.SemaphoreType.DMA((BUFFERS,)),
]


def params(megabytes):
    return pltpu.CompilerParams(
        dimension_semantics=("arbitrary",), vmem_limit_bytes=megabytes * 1024 * 1024
    )


def cost(megabytes):
    return pl.CostEstimate(flops=10**10, bytes_accessed=megabytes * 10**6, transcendentals=0)


def first_half(target, odd, a, p, halos):
    found = pl.pallas_call(
        first_kernel,
        grid=(E_DEV // GROUP,),
        in_specs=[
            SMEM,
            SMEM,
            pl.BlockSpec((PAIRS, GROUP, SQUARE), lambda i: (0, i, 0)),
            VMEM, HBM, HBM, HBM, HBM,
        ],
        out_specs=[HBM] * (3 + len(PACKS)),
        out_shape=[
            jax.ShapeDtypeStruct((E_DEV, BLOCK, PAIRS * 128), jnp.bfloat16),
            jax.ShapeDtypeStruct((E_DEV, BLOCK, BLOCK), jnp.bfloat16),
            jax.ShapeDtypeStruct((4 * FACE, BLOCK, 128), jnp.bfloat16),
        ]
        + PACKS,
        scratch_shapes=SUMS
        + [
            pltpu.VMEM((PAIRS, E_DEV + 1, ROWS, 128), jnp.bfloat16),
            pltpu.VMEM((E_DEV + 1, BLOCK, PAIRS * 128), jnp.bfloat16),
            pltpu.VMEM((PAIRS * GROUP * PITCH + 8, 128), jnp.float32),
            pltpu.VMEM((E_DEV, 128, 256), jnp.bfloat16),
            pltpu.VMEM((E_DEV, BLOCK, BLOCK), jnp.bfloat16),
            pltpu.VMEM((4 * FACE, BLOCK, 128), jnp.bfloat16),
            pltpu.VMEM((4, FACE, SQUARE), jnp.bfloat16),
            pltpu.SemaphoreType.DMA((E_DEV // GROUP + 6,)),
        ],
        compiler_params=params(62),
        cost_estimate=cost(60),
        name="first_half",
    )(target, odd, a, p, *halos)
    return found[0], found[1], found[2], found[3:]


def second_half(target, lefts, q, qh):
    return pl.pallas_call(
        second_kernel,
        grid=(E_DEV // GROUP,),
        in_specs=[SMEM, HBM, Q_SPEC, HBM],
        out_specs=[HBM] * len(PACKS),
        out_shape=PACKS,
        scratch_shapes=SUMS
        + [
            pltpu.VMEM((E_DEV, BLOCK, BLOCK), jnp.bfloat16),
            pltpu.VMEM((4 * FACE, BLOCK, 128), jnp.bfloat16),
            pltpu.SemaphoreType.DMA((2,)),
        ],
        compiler_params=params(48),
        cost_estimate=cost(60),
        name="second_half",
    )(target, lefts, q, qh)


def faces(p):
    brick = p.reshape(EZ, EY, EX, SQUARE)
    found = []
    for axis, dim in (("dom", 1), ("slab", 0)):
        size = lax.axis_size(axis)
        even = lax.axis_index(axis) % 2 == 0
        length = brick.shape[dim]
        last = lax.slice_in_dim(brick, length - 1, length, axis=dim).reshape(FACE, SQUARE)
        first = lax.slice_in_dim(brick, 0, 1, axis=dim).reshape(FACE, SQUARE)
        near = [(i, i ^ 1) for i in range(size)]
        far = [(i, (i + 1 ^ 1) - 1) for i in range(1, size - 1)]
        found.append(lax.ppermute(jnp.where(even, last, first), axis, near))
        found.append(lax.ppermute(jnp.where(even, first, last), axis, far))
    return found


def sum_places(dest_rank, dest_block):
    me = lax.axis_index("dom")
    away = dest_rank.reshape(-1) ^ me
    block = dest_block.reshape(-1)
    dx = away % SIDE
    dy = away // SIDE
    which = block // (2 * PART)
    part = (block // PART) % 2
    place = jnp.where(which == 0, dx, dy)
    other = jnp.where(which == 0, dy, dx)
    slot = (SLOT_OF >> (4 * (2 * place + part))) & 7
    return ((which * (SLOTS // 2) + slot) * SIDE + other) * PART + block % PART


def pair_perms():
    return [
        [[(i, i ^ (swap * stride)) for i in range(OWNERS)] for swap in (1, 3)]
        for stride in (1, SIDE)
    ]


def added(*parts):
    total = parts[0].astype(jnp.float32)
    for part in parts[1:]:
        total = total + part.astype(jnp.float32)
    return total


def join(keep, arrived):
    return added(keep, arrived).astype(jnp.bfloat16)


def exchange(halves):
    along_x, along_y = pair_perms()
    sets = ((0, along_x, along_y), (5, along_y, along_x))

    def send(pair, perms):
        return [lax.ppermute(v, "dom", perm) for v, perm in zip(pair, perms)]

    first = [
        lax.optimization_barrier([send(packs[at : at + 2], one) for at, one, _ in sets])
        for packs in halves
    ]
    second = []
    for packs, arrived in zip(halves, first):
        row = []
        for (at, one, _), (near, far) in zip(sets, arrived):
            joined = join(packs[at + 2][0], far[0]), join(packs[at + 3][0], near[0])
            row.append(send(joined, one))
        second.append(lax.optimization_barrier(row))
    shape = (SIDE, PART, HALF, 128)
    sums = [[], []]
    for packs, one, two in zip(halves, first, second):
        for n, ((at, _, _), (n1, f1), (n2, f2)) in enumerate(zip(sets, one, two)):
            own = packs[at + 4]
            sums[n].append(
                (added(own[0], n1[1], f2).reshape(shape), added(own[1], f1[1], n2).reshape(shape))
            )
    third, kept = [], []
    for (_, _, two), parts in zip(sets, sums):
        p0, p1 = ([jnp.stack([h[p][n] for h in parts]) for n in range(SIDE)] for p in range(2))
        q0, q1 = ([v.astype(jnp.bfloat16) for v in w] for w in (p0, p1))
        kept.append((p0[0], p1[0], q1[1], q0[3]))
        third.append(send((jnp.stack([q0[2], q0[1]]), jnp.stack([q1[2], q1[3]])), two))
    third = lax.optimization_barrier(third)
    joined = [
        (join(keep_near, far[0]), join(keep_far, near[0]))
        for (_, _, keep_near, keep_far), (near, far) in zip(kept, third)
    ]
    joined, third = lax.optimization_barrier((joined, third))
    found = []
    for (_, _, two), (own0, own1, _, _), (n1, f1), pair in zip(sets, kept, third, joined):
        n2, f2 = send(pair, two)
        found += [added(own0, n1[1]), added(own1, f1[1]), f2, n2]
    return found


def finish_kernel(*refs):
    *ins, out_ref, scratch, bases, flat, in_sems, out_sems = refs
    places = [4 * (n // 2) + n % 2 for n in range(4)]
    fetches = [
        pltpu.make_async_copy(ins[at], bases.at[n], in_sems.at[n]) for n, at in enumerate(places)
    ]
    for fetch in fetches:
        fetch.start()
    stores = []
    for n, at in enumerate(places):
        fetches[n].wait()
        for half in range(2):
            total = added(bases[n, half], ins[at + 2][half])
            for c in range(PART):
                scratch[c * FLAT_PITCH : c * FLAT_PITCH + HALF, :] = total[c]
            for u in range(HALF):
                t = half * HALF + u
                flat[n, :, t * 128 : (t + 1) * 128] = scratch[pl.ds(u, PART, stride=FLAT_PITCH), :]
        store = pltpu.make_async_copy(
            flat.at[n], out_ref.at[pl.ds(n * PART, PART)], out_sems.at[n]
        )
        store.start()
        stores.append(store)
    for store in stores:
        store.wait()


def finish(parts):
    return pl.pallas_call(
        finish_kernel,
        in_specs=[HBM, HBM, VMEM, VMEM] * 2,
        out_specs=HBM,
        out_shape=jax.ShapeDtypeStruct((CB_DEV, SQUARE), jnp.float32),
        scratch_shapes=[
            pltpu.VMEM((PART * FLAT_PITCH + 8, 128), jnp.float32),
            pltpu.VMEM((4, 2, PART, HALF, 128), jnp.float32),
            pltpu.VMEM((4, PART, SQUARE), jnp.float32),
            pltpu.SemaphoreType.DMA((4,)),
            pltpu.SemaphoreType.DMA((4,)),
        ],
        name="finish",
    )(*parts)


def on_device(a_blocks, p_blocks, dest_rank, dest_block):
    halos = faces(p_blocks)
    target = sum_places(dest_rank, dest_block)
    odd = jnp.stack([lax.axis_index(axis) % 2 for axis in ("dom", "slab")])
    a = jnp.swapaxes(a_blocks, 0, 1)
    q, lefts, qh, first = first_half(target, odd, a, p_blocks, halos)
    second = second_half(target, lefts, q, qh)
    return finish(exchange((first, second)))


def solution(mesh):
    return jax.shard_map(
        on_device,
        mesh=mesh,
        in_specs=(
            P(("slab", "dom"), None, None),
            P(("slab", "dom"), None),
            P(("slab", "dom"), None),
            P(("slab", "dom"), None),
        ),
        out_specs=P(("slab", "dom"), None),
        check_vma=False,
    )
```

```python
import jax
import jax.numpy as jnp
from jax import lax
from jax.experimental import pallas as pl
from jax.experimental.pallas import tpu as pltpu
from jax.sharding import PartitionSpec as P

BLOCK = 64
PAIRS = 7
EX = 8
EY = 4
EZ = 4
E_DEV = EX * EY * EZ
CB_DEV = 128
SQUARE = BLOCK * BLOCK
ROWS = SQUARE // 128
HALF = ROWS // 2
PITCH = 33
FLAT_PITCH = 17
GROUP = 16
FACE = 32
SIDE = 4
OWNERS = SIDE * SIDE
PART = CB_DEV // 4
SLOT = SIDE * PART
SLOTS = OWNERS * CB_DEV // SLOT
BUFFERS = 4
PLACES = 4096
SLOT_OF = 0x35204176


def spread_rows(flat, scratch, base):
    for t in range(ROWS):
        scratch[pl.ds(base + t, GROUP, stride=PITCH), :] = flat(t).astype(jnp.float32)


def piece(scratch, index):
    return scratch[pl.ds(index * PITCH, ROWS), :]


def clear(acc):
    def body(i, _):
        acc[pl.ds(i * 16, 16)] = jnp.zeros((16, HALF, 128), jnp.float32)
        return 0

    lax.fori_loop(0, OWNERS * CB_DEV // 16, body, 0)


def spread_weights(ref, base, rows, weights, slot0, lefts):
    low = lax.broadcasted_iota(jnp.int32, (ROWS, 128), 1) < BLOCK
    low2 = lax.broadcasted_iota(jnp.int32, (BLOCK, 128), 1) < BLOCK
    r = lax.broadcasted_iota(jnp.int32, (BLOCK, BLOCK), 0)
    c = lax.broadcasted_iota(jnp.int32, (BLOCK, BLOCK), 1)
    place = (c == (r % 2) * ROWS + r // 2).astype(jnp.float32).astype(jnp.bfloat16)
    r = lax.broadcasted_iota(jnp.int32, (BLOCK, 128), 0)
    c = lax.broadcasted_iota(jnp.int32, (BLOCK, 128), 1)
    v = (r // HALF) % 2
    lane = v * BLOCK + 2 * ((r // ROWS) * HALF + r % HALF) + v
    pick = (c == lane).astype(jnp.float32).astype(jnp.bfloat16)
    spread_rows(lambda t: ref[pl.ds(base, GROUP), t * 128 : (t + 1) * 128], rows, 0)
    for i in range(0, GROUP, 2):
        ordered = []
        for j in (i, i + 1):
            own = piece(rows, j)
            turned = pltpu.roll(own, BLOCK, 1)
            ordered.append(
                jnp.concatenate(
                    [jnp.where(low, own, turned), jnp.where(low, turned, own)], axis=0
                ).astype(jnp.bfloat16)
            )
            if lefts is not None:
                stacked = jnp.concatenate([own, turned], axis=0)
                left = lax.dot_general(
                    pick, stacked.astype(jnp.bfloat16), (((1,), (1,)), ((), ())),
                    preferred_element_type=jnp.float32,
                )
                lefts[base + j] = left.astype(jnp.bfloat16)
        placed = jnp.dot(
            place, jnp.concatenate(ordered, axis=1), preferred_element_type=jnp.float32
        )
        for j in (0, 1):
            twice = placed[:, j * 128 : (j + 1) * 128]
            at_low = jnp.where(low2, twice, 0.0).astype(jnp.bfloat16)
            at_high = jnp.where(low2, 0.0, twice).astype(jnp.bfloat16)
            weights[slot0 + i + j, :BLOCK, :128] = at_low
            weights[slot0 + i + j, :BLOCK, 128:] = at_high
            weights[slot0 + i + j, BLOCK:, :128] = at_high
            weights[slot0 + i + j, BLOCK:, 128:] = at_low


def first_kernel(target_ref, a_ref, p_ref, *refs):
    halos, (q_out, left_out, qh_out), outs = refs[:4], refs[4:7], refs[7:17]
    acc, stage, drain_sems, couples, q, rows, weights, left_ref, qh_ref, near, sems = refs[17:]
    step = pl.program_id(0)

    fetches = [
        pltpu.make_async_copy(ref, near.at[f], sems.at[E_DEV // GROUP + 2 + f])
        for f, ref in enumerate(halos)
    ]

    @pl.when(step == 0)
    def _clear():
        for fetch in fetches:
            fetch.start()
        clear(acc)

    start = pl.multiple_of(step * GROUP, GROUP)
    spread_weights(p_ref, start, rows, weights, start, left_ref)
    for k in range(PAIRS):
        spread_rows(
            lambda t: a_ref[k, :, t * 128 : (t + 1) * 128], rows, k * (GROUP * PITCH)
        )

    def lay(i, _):
        for k in range(PAIRS):
            couples[k, step * GROUP + i] = piece(rows, k * GROUP + i).astype(jnp.bfloat16)
        return 0

    lax.fori_loop(0, GROUP, lay, 0, unroll=4)

    @pl.when(step == pl.num_programs(0) - 1)
    def _multiply():
        plane = EX * EY

        def copy(n):
            span = pl.ds(n * GROUP, GROUP)
            return pltpu.make_async_copy(q.at[span], q_out.at[span], sems.at[n])

        lefts_away = pltpu.make_async_copy(left_ref, left_out, sems.at[E_DEV // GROUP])
        faces_away = pltpu.make_async_copy(qh_ref, qh_out, sems.at[E_DEV // GROUP + 1])
        lefts_away.start()
        behind = plane // GROUP

        for z in range(EZ):
            for g in range(plane // GROUP):
                base = z * plane + g * GROUP
                def neighbour(i, _):
                    j = base + i
                    x = j % EX
                    y = (j // EX) % EY
                    inside = (
                        None, x < EX - 1, x > 0, y < EY - 1, y > 0,
                        z < EZ - 1 or None, z > 0 or None,
                    )
                    away = (0, 1, -1, EX, -EX, plane, -plane)
                    here = [k for k in range(PAIRS) if k < 5 or inside[k]]
                    owners = [
                        j + away[k] if inside[k] is None or k >= 5
                        else jnp.where(inside[k], j + away[k], E_DEV)
                        for k in here
                    ]
                    left = jnp.concatenate(
                        [couples[k, e] for k, e in zip(here, owners)], axis=0
                    )
                    found = jnp.dot(left, weights[j], preferred_element_type=jnp.float32)
                    found = found.astype(jnp.bfloat16)
                    for n, (k, e) in enumerate(zip(here, owners)):
                        own = found[n * ROWS : (n + 1) * ROWS]
                        q[e, :ROWS, k * 128 : (k + 1) * 128] = own[:, :128]
                        q[e, ROWS:, k * 128 : (k + 1) * 128] = own[:, 128:]
                    return 0

                lax.fori_loop(0, GROUP, neighbour, 0, unroll=GROUP)
                if base // GROUP >= behind:
                    copy(base // GROUP - behind).start()
        for n in range(E_DEV // GROUP - behind, E_DEV // GROUP):
            copy(n).start()

        odd = target_ref[0] // PLACES
        dom_odd, slab_odd = odd % 2, odd // 2
        sides = (1 - dom_odd, dom_odd, 3 - slab_odd, 2 + slab_odd)
        for n, f in enumerate(sides):
            fetches[n].wait()
            for g in range(FACE // GROUP):
                spread_weights(near.at[n], g * GROUP, rows, weights, f * FACE + g * GROUP, None)

        def face_pair(n, _):
            column = n // EX * plane + n % EX
            elements = (column, column + plane - EX, n, n + E_DEV - plane)
            for f, e in enumerate(elements):
                found = jnp.dot(
                    couples[3 + f, e], weights[f * FACE + n], preferred_element_type=jnp.float32
                ).astype(jnp.bfloat16)
                qh_ref[f * FACE + n, :ROWS, :] = found[:, :128]
                qh_ref[f * FACE + n, ROWS:, :] = found[:, 128:]
            return 0

        lax.fori_loop(0, FACE, face_pair, 0, unroll=8)
        faces_away.start()

        def terms(n, _):
            add_face_terms(n, 0, target_ref, left_ref, qh_ref, acc)
            add_terms(n, 0, target_ref, left_ref, q.at[pl.ds(n * GROUP, GROUP)], acc)
            return 0

        lax.fori_loop(0, E_DEV // GROUP, terms, 0)
        drain(acc, stage, drain_sems, outs)
        for n in range(E_DEV // GROUP):
            copy(n).wait()
        lefts_away.wait()
        faces_away.wait()


def add_terms(step, half, target_ref, lefts, q_ref, acc):
    low = lax.broadcasted_iota(jnp.int32, (HALF, PAIRS * 128), 1) % 128 < BLOCK

    def element(i, _):
        e = step * GROUP + i
        x = e % EX
        y = (e // EX) % EY
        z = e // (EX * EY)
        inside = (None, x > 0, x < EX - 1, y > 0, y < EY - 1, z > 0, z < EZ - 1)
        both = jnp.dot(
            lefts[e, half * ROWS : (half + 1) * ROWS, :], q_ref[i],
            preferred_element_type=jnp.float32,
        )
        terms = jnp.where(low, both[:HALF], both[HALF:])
        terms = terms.astype(jnp.bfloat16).astype(jnp.float32)
        for k in range(PAIRS):
            target = target_ref[e * PAIRS + k] % PLACES
            if inside[k] is not None:
                target = jnp.where(inside[k], target, OWNERS * CB_DEV)
            acc[target] += terms[:, k * 128 : (k + 1) * 128]
        return 0

    lax.fori_loop(0, GROUP, element, 0, unroll=GROUP)


def add_face_terms(step, half, target_ref, lefts, qh_ref, acc):
    low = lax.broadcasted_iota(jnp.int32, (HALF, 128), 1) < BLOCK
    plane = EX * EY
    face = step // (FACE // GROUP)

    def pair(i, _):
        n = step % (FACE // GROUP) * GROUP + i
        column = n // EX * plane + n % EX
        e = jnp.where(
            face < 2, column + face * (plane - EX), n + (face - 2) * (E_DEV - plane)
        )
        both = jnp.dot(
            lefts[e, half * ROWS : (half + 1) * ROWS, :], qh_ref[step * GROUP + i],
            preferred_element_type=jnp.float32,
        )
        term = jnp.where(low, both[:HALF], both[HALF:])
        target = target_ref[e * PAIRS + 3 + face] % PLACES
        acc[target] += term.astype(jnp.bfloat16).astype(jnp.float32)
        return 0

    lax.fori_loop(0, GROUP, pair, 0, unroll=GROUP)


def drain(acc, stage, sems, outs):
    places = []
    for out in outs:
        places += [out.at[i] for i in range(out.shape[0])]
    copies = []
    for n in range(SLOTS):
        buffer = n % BUFFERS
        if n >= BUFFERS:
            copies[n - BUFFERS].wait()

        def cast(i, _):
            blocks = acc[pl.ds(n * SLOT + i * 16, 16)]
            stage[buffer, pl.ds(i * 16, 16)] = blocks.astype(jnp.bfloat16)
            return 0

        lax.fori_loop(0, SLOT // 16, cast, 0)
        copy = pltpu.make_async_copy(stage.at[buffer], places[n], sems.at[buffer])
        copy.start()
        copies.append(copy)
    for copy in copies[-BUFFERS:]:
        copy.wait()


def second_kernel(target_ref, left_in, q_ref, qh_in, *refs):
    outs = refs[:10]
    acc, stage, drain_sems, left_ref, qh_ref, sems = refs[10:]
    step = pl.program_id(0)

    @pl.when(step == 0)
    def _clear():
        lefts = pltpu.make_async_copy(left_in, left_ref, sems.at[0])
        faces = pltpu.make_async_copy(qh_in, qh_ref, sems.at[1])
        lefts.start()
        faces.start()
        clear(acc)
        lefts.wait()
        faces.wait()

    add_face_terms(step, 1, target_ref, left_ref, qh_ref, acc)
    add_terms(step, 1, target_ref, left_ref, q_ref, acc)

    @pl.when(step == pl.num_programs(0) - 1)
    def _drain():
        drain(acc, stage, drain_sems, outs)


VMEM = pl.BlockSpec(memory_space=pltpu.VMEM)
SMEM = pl.BlockSpec(memory_space=pltpu.SMEM)
HBM = pl.BlockSpec(memory_space=pl.ANY)
Q_SPEC = pl.BlockSpec((GROUP, BLOCK, PAIRS * 128), lambda i: (i, 0, 0))
PACKS = [
    jax.ShapeDtypeStruct((n, SLOT, HALF, 128), jnp.bfloat16) for n in (2, 2, 1, 1, 2) * 2
]
SUMS = [
    pltpu.VMEM((OWNERS * CB_DEV + 1, HALF, 128), jnp.float32),
    pltpu.VMEM((BUFFERS, SLOT, HALF, 128), jnp.bfloat16),
    pltpu.SemaphoreType.DMA((BUFFERS,)),
]


def params(megabytes):
    return pltpu.CompilerParams(
        dimension_semantics=("arbitrary",), vmem_limit_bytes=megabytes * 1024 * 1024
    )


def cost(megabytes):
    return pl.CostEstimate(flops=10**10, bytes_accessed=megabytes * 10**6, transcendentals=0)


def first_half(target, a, p, halos):
    found = pl.pallas_call(
        first_kernel,
        grid=(E_DEV // GROUP,),
        in_specs=[
            SMEM,
            pl.BlockSpec((PAIRS, GROUP, SQUARE), lambda i: (0, i, 0)),
            VMEM, HBM, HBM, HBM, HBM,
        ],
        out_specs=[HBM] * (3 + len(PACKS)),
        out_shape=[
            jax.ShapeDtypeStruct((E_DEV, BLOCK, PAIRS * 128), jnp.bfloat16),
            jax.ShapeDtypeStruct((E_DEV, BLOCK, BLOCK), jnp.bfloat16),
            jax.ShapeDtypeStruct((4 * FACE, BLOCK, 128), jnp.bfloat16),
        ]
        + PACKS,
        scratch_shapes=SUMS
        + [
            pltpu.VMEM((PAIRS, E_DEV + 1, ROWS, 128), jnp.bfloat16),
            pltpu.VMEM((E_DEV + 1, BLOCK, PAIRS * 128), jnp.bfloat16),
            pltpu.VMEM((PAIRS * GROUP * PITCH + 8, 128), jnp.float32),
            pltpu.VMEM((E_DEV, 128, 256), jnp.bfloat16),
            pltpu.VMEM((E_DEV, BLOCK, BLOCK), jnp.bfloat16),
            pltpu.VMEM((4 * FACE, BLOCK, 128), jnp.bfloat16),
            pltpu.VMEM((4, FACE, SQUARE), jnp.bfloat16),
            pltpu.SemaphoreType.DMA((E_DEV // GROUP + 6,)),
        ],
        compiler_params=params(58),
        cost_estimate=cost(60),
        name="first_half",
    )(target, a, p, *halos)
    return found[0], found[1], found[2], found[3:]


def second_half(target, lefts, q, qh):
    return pl.pallas_call(
        second_kernel,
        grid=(E_DEV // GROUP,),
        in_specs=[SMEM, HBM, Q_SPEC, HBM],
        out_specs=[HBM] * len(PACKS),
        out_shape=PACKS,
        scratch_shapes=SUMS
        + [
            pltpu.VMEM((E_DEV, BLOCK, BLOCK), jnp.bfloat16),
            pltpu.VMEM((4 * FACE, BLOCK, 128), jnp.bfloat16),
            pltpu.SemaphoreType.DMA((2,)),
        ],
        compiler_params=params(48),
        cost_estimate=cost(60),
        name="second_half",
    )(target, lefts, q, qh)


def faces(p):
    brick = p.reshape(EZ, EY, EX, SQUARE)
    found = []
    for axis, dim in (("dom", 1), ("slab", 0)):
        size = lax.axis_size(axis)
        even = lax.axis_index(axis) % 2 == 0
        length = brick.shape[dim]
        last = lax.slice_in_dim(brick, length - 1, length, axis=dim).reshape(FACE, SQUARE)
        first = lax.slice_in_dim(brick, 0, 1, axis=dim).reshape(FACE, SQUARE)
        near = [(i, i ^ 1) for i in range(size)]
        far = [(i, (i + 1 ^ 1) - 1) for i in range(1, size - 1)]
        found.append(lax.ppermute(jnp.where(even, last, first), axis, near))
        found.append(lax.ppermute(jnp.where(even, first, last), axis, far))
    return found


def sum_places(dest_rank, dest_block):
    me = lax.axis_index("dom")
    odd = me % 2 + 2 * (lax.axis_index("slab") % 2)
    away = dest_rank.reshape(-1) ^ me
    block = dest_block.reshape(-1)
    dx = away % SIDE
    dy = away // SIDE
    which = block // (2 * PART)
    part = (block // PART) % 2
    place = jnp.where(which == 0, dx, dy)
    other = jnp.where(which == 0, dy, dx)
    slot = (SLOT_OF >> (4 * (2 * place + part))) & 7
    found = ((which * (SLOTS // 2) + slot) * SIDE + other) * PART + block % PART
    return found + odd * PLACES


def pair_perms():
    return [
        [[(i, i ^ (swap * stride)) for i in range(OWNERS)] for swap in (1, 3)]
        for stride in (1, SIDE)
    ]


def added(*parts):
    total = parts[0].astype(jnp.float32)
    for part in parts[1:]:
        total = total + part.astype(jnp.float32)
    return total


def join(keep, arrived):
    return added(keep, arrived).astype(jnp.bfloat16)


def exchange(halves):
    along_x, along_y = pair_perms()
    sets = ((0, along_x, along_y), (5, along_y, along_x))

    def send(pair, perms):
        return [lax.ppermute(v, "dom", perm) for v, perm in zip(pair, perms)]

    first = [
        lax.optimization_barrier([send(packs[at : at + 2], one) for at, one, _ in sets])
        for packs in halves
    ]
    second = []
    for packs, arrived in zip(halves, first):
        row = []
        for (at, one, _), (near, far) in zip(sets, arrived):
            joined = join(packs[at + 2][0], far[0]), join(packs[at + 3][0], near[0])
            row.append(send(joined, one))
        second.append(lax.optimization_barrier(row))
    shape = (SIDE, PART, HALF, 128)
    sums = [[], []]
    for packs, one, two in zip(halves, first, second):
        for n, ((at, _, _), (n1, f1), (n2, f2)) in enumerate(zip(sets, one, two)):
            own = packs[at + 4]
            sums[n].append(
                (added(own[0], n1[1], f2).reshape(shape), added(own[1], f1[1], n2).reshape(shape))
            )
    third, kept = [], []
    for half in range(2):
        row, keep = [], []
        for (_, _, two), parts in zip(sets, sums):
            p0, p1 = parts[half]
            q0, q1 = p0.astype(jnp.bfloat16), p1.astype(jnp.bfloat16)
            keep.append((p0[0], p1[0], q1[1], q0[3]))
            row.append(send((jnp.stack([q0[2], q0[1]]), jnp.stack([q1[2], q1[3]])), two))
        third.append(lax.optimization_barrier(row))
        kept.append(keep)
    joined = []
    for n in range(2):
        near = [join(keep[n][2], row[n][1][0]) for keep, row in zip(kept, third)]
        far = [join(keep[n][3], row[n][0][0]) for keep, row in zip(kept, third)]
        joined.append((jnp.stack(near), jnp.stack(far)))
    joined, third = lax.optimization_barrier((joined, third))
    found = []
    for n, ((_, _, two), pair) in enumerate(zip(sets, joined)):
        n2, f2 = send(pair, two)
        for part in range(2):
            base = [added(keep[n][part], row[n][part][1]) for keep, row in zip(kept, third)]
            found.append(jnp.stack(base))
        found += [f2, n2]
    return found


def finish_kernel(*refs):
    *ins, out_ref, scratch, bases, flat, in_sems, out_sems = refs
    places = [4 * (n // 2) + n % 2 for n in range(4)]
    fetches = [
        pltpu.make_async_copy(ins[at], bases.at[n], in_sems.at[n]) for n, at in enumerate(places)
    ]
    for fetch in fetches:
        fetch.start()
    stores = []
    for n, at in enumerate(places):
        fetches[n].wait()
        for half in range(2):
            total = added(bases[n, half], ins[at + 2][half])
            for c in range(PART):
                scratch[c * FLAT_PITCH : c * FLAT_PITCH + HALF, :] = total[c]
            for u in range(HALF):
                t = half * HALF + u
                flat[n, :, t * 128 : (t + 1) * 128] = scratch[pl.ds(u, PART, stride=FLAT_PITCH), :]
        store = pltpu.make_async_copy(
            flat.at[n], out_ref.at[pl.ds(n * PART, PART)], out_sems.at[n]
        )
        store.start()
        stores.append(store)
    for store in stores:
        store.wait()


def finish(parts):
    return pl.pallas_call(
        finish_kernel,
        in_specs=[HBM, HBM, VMEM, VMEM] * 2,
        out_specs=HBM,
        out_shape=jax.ShapeDtypeStruct((CB_DEV, SQUARE), jnp.float32),
        scratch_shapes=[
            pltpu.VMEM((PART * FLAT_PITCH + 8, 128), jnp.float32),
            pltpu.VMEM((4, 2, PART, HALF, 128), jnp.float32),
            pltpu.VMEM((4, PART, SQUARE), jnp.float32),
            pltpu.SemaphoreType.DMA((4,)),
            pltpu.SemaphoreType.DMA((4,)),
        ],
        name="finish",
    )(*parts)


def on_device(a_blocks, p_blocks, dest_rank, dest_block):
    halos = faces(p_blocks)
    target = sum_places(dest_rank, dest_block)
    a = jnp.swapaxes(a_blocks, 0, 1)
    q, lefts, qh, first = first_half(target, a, p_blocks, halos)
    second = second_half(target, lefts, q, qh)
    return finish(exchange((first, second)))


def solution(mesh):
    return jax.shard_map(
        on_device,
        mesh=mesh,
        in_specs=(
            P(("slab", "dom"), None, None),
            P(("slab", "dom"), None),
            P(("slab", "dom"), None),
            P(("slab", "dom"), None),
        ),
        out_specs=P(("slab", "dom"), None),
        check_vma=False,
    )
```
